256 devices in a mesh: region: 8 (over x, core), sector: 32 (over z, y).
Axes of the slice: x: 4, y: 4, z: 8, core: 2. Of those that a mesh axis runs over, the one named last changes fastest.
Arguments:
- start_state: bfloat16 [8, 128, 128, 4, 128], P('region', 'sector'), may hold values from -6 to 6
- left_env: bfloat16 [8, 128, 16, 128, 128], P('region', 'sector'), may hold values from -0.125 to 0.125
- right_env: bfloat16 [8, 128, 16, 128, 128], P('region', 'sector'), may hold values from -0.5 to 0.5
- mpo_tensor: bfloat16 [16, 4, 4, 16], replicated, may hold values from -0.75 to 0.75
- decay: float32 [8, 128, 128], P('region', 'sector'), may hold values from 0.15 to 1
- energy_terms: float32 [8, 128, 128], P('region', 'sector'), may hold values from -1.2 to 1.2
- live_count: int32 [8, 32], P('region', 'sector'), may hold values from 1 to 4, as said below
Outputs:
- state_out: bfloat16 [8, 128, 128, 4, 128], P('region', 'sector')
- density: float32 [8, 128, 128, 128], P('region', 'sector')
- energy: float32 [8], P('region')
The draws below stay inside these ranges and needn't reach their ends.
Inputs may be any that keep to these rules, and one draw needn't show every extreme that they name: `live_count`: each device's live blocks fill its first slots; some device holds 4 live blocks.
All inputs are finite; a program needn't handle non-finite values.
Results may differ from the reference program's by a relative error of at most 0.0055.
The reference program's roundings to bfloat16 on the way (of `contract_right` and `contract_mpo`) count: a program that leaves them out, or rounds other values in their place, can miss the bound.
Values may be sent and summed in bfloat16 or wider, within the bound.
No kernel may reach another device: no remote copies, remote signals or barrier semaphores. Data moves between devices by JAX's collectives and lax.ppermute only.
A program may use at most 64 MiB of HBM per device.

```python
import math
import jax
import jax.numpy as jnp
from jax import lax

BLK = 128
PHYS = 4
CHAN = 16
SLOTS = 4
DAV = 2
LATTICE_PARTS = 8
SECTORS = 32
BLOCKS = 128


def draw_decay(key, part):
    stochastic_seeds = jax.random.split(key, 5)
    array_dimensions = (LATTICE_PARTS, BLOCKS, BLK)
    slow_share = 0.5
    channel_pick = jax.random.uniform(stochastic_seeds[0], (1, BLOCKS, BLK), jnp.float32)
    is_slow = channel_pick < slow_share
    rate_draw = jax.random.uniform(stochastic_seeds[1], (1, BLOCKS, BLK), jnp.float32, 0.2, 1.2)
    tardy_lines = jnp.exp(-rate_draw / LATTICE_PARTS) * jnp.ones(array_dimensions, jnp.float32)
    fast_rows = jax.random.uniform(stochastic_seeds[2], array_dimensions, jnp.float32, 0.3, 0.7)
    spurt_extent = jax.random.uniform(stochastic_seeds[3], array_dimensions, jnp.float32) < 1.5 / LATTICE_PARTS
    spurt_ceiling = jax.random.uniform(stochastic_seeds[4], array_dimensions, jnp.float32, 0.5, 0.8)
    tardy_lines = jnp.where(spurt_extent, tardy_lines * spurt_ceiling, tardy_lines)
    return jnp.where(is_slow, tardy_lines, fast_rows).astype(jnp.float32)


def draw_live_count(key, part):
    stochastic_seeds = jax.random.split(key, 3)
    first_draw = jax.random.randint(stochastic_seeds[0], (LATTICE_PARTS, SECTORS), 0, SLOTS)
    second_draw = jax.random.randint(stochastic_seeds[1], (LATTICE_PARTS, SECTORS), 0, SLOTS)
    counts = 1 + first_draw * second_draw // max(SLOTS - 1, 1)
    chosen = jax.random.randint(stochastic_seeds[2], (), 0, LATTICE_PARTS * SECTORS)
    flat_counts = jnp.where(jnp.arange(LATTICE_PARTS * SECTORS, dtype=jnp.int32) == chosen, SLOTS, counts.reshape(-1))
    return flat_counts.reshape(LATTICE_PARTS, SECTORS).astype(jnp.int32)


def steps_of(rng, extent, cuts, low, largest):
    def one(position, blocks):
        steps = jax.random.uniform(jax.random.fold_in(jax.random.fold_in(rng, 6), position), (blocks,), jnp.float32, low / len(cuts), largest / len(cuts))
        return jnp.repeat(jnp.exp(steps), extent[position] // blocks).reshape((-1,) + (1,) * (len(extent) - position - 1))

    factor_of = one(*cuts[0])
    for cut in cuts[1:]:
        factor_of = factor_of * one(*cut)
    return factor_of


def bell_draw(rng, shape, width, limit, shards=(), kind=jnp.bfloat16):
    array = width * jax.random.normal(rng, shape, jnp.float32)
    if shards:
        array = array * steps_of(rng, shape, shards, -0.22, 0.18)
    return jnp.clip(array, -limit, limit).astype(kind)


def setup_inputs(seed: int = 0) -> dict:
    key_list = jax.random.split(jax.random.key(seed), 8)
    return {
        "start_state": bell_draw(key_list[0], (LATTICE_PARTS, BLOCKS, BLK, PHYS, BLK), 1.0, 6.0, ((0, 8), (1, 32))),
        "left_env": bell_draw(key_list[1], (LATTICE_PARTS, BLOCKS, CHAN, BLK, BLK), (CHAN * BLK) ** -0.5, 0.125, ((0, 8), (1, 32))),
        "right_env": bell_draw(key_list[2], (LATTICE_PARTS, BLOCKS, CHAN, BLK, BLK), BLK ** -0.5, 0.5, ((0, 8), (1, 32))),
        "mpo_tensor": bell_draw(key_list[3], (CHAN, PHYS, PHYS, CHAN), (PHYS * CHAN) ** -0.5, 0.75),
        "decay": draw_decay(jax.random.fold_in(key_list[7], 71), 0),
        "energy_terms": bell_draw(key_list[5], (LATTICE_PARTS, BLOCKS, BLK), 0.2, 1.2, ((0, 8), (1, 32)), jnp.float32),
        "live_count": draw_live_count(jax.random.fold_in(key_list[7], 71), 0),
    }


epsilon = 1e-06

def apply_block(vector, left_part, right_part, mpo_tensor, offset):
    vector_wide = vector.astype(jnp.float32)
    contract_right = jnp.einsum('asc,wcb->aswb', vector_wide, right_part.astype(jnp.float32)).astype(jnp.bfloat16)
    contract_mpo = jnp.einsum('vstw,atwb->asvb', mpo_tensor.astype(jnp.float32), contract_right.astype(jnp.float32)).astype(jnp.bfloat16)
    applied = jnp.einsum('vac,csvb->asb', left_part.astype(jnp.float32), contract_mpo.astype(jnp.float32))
    return applied + offset[:, None, None] * vector_wide

def accumulate(running, row_pair):
    return (row_pair[0] * running + row_pair[1], running)

def reference(start_state, left_env, right_env, mpo_tensor, decay, energy_terms, live_count):
    initial = jnp.zeros((BLOCKS, BLK), jnp.float32)
    unused, offsets = lax.scan(accumulate, initial, (decay, energy_terms))
    scale = math.sqrt(BLOCKS * BLK * PHYS * BLK)

    def region_solve(region_index):
        previous = jnp.maximum(region_index - 1, 0).astype(jnp.int32)
        left_part = lax.dynamic_index_in_dim(left_env, previous, 0, keepdims=False)
        right_part = lax.dynamic_index_in_dim(right_env, region_index, 0, keepdims=False)
        starting = lax.dynamic_index_in_dim(start_state, region_index, 0, keepdims=False)
        offset_rows = lax.dynamic_index_in_dim(offsets, region_index, 0, keepdims=False)
        counts = lax.dynamic_index_in_dim(live_count, region_index, 0, keepdims=False)
        slot_ids = jnp.arange(BLOCKS, dtype=jnp.int32)
        live_mask = slot_ids % SLOTS < counts[slot_ids // SLOTS]

        def operate(vector_bf):

            def count_per_block(block_items):
                vector, left_one, right_one, offset_one, is_active_region = block_items
                return lax.cond(is_active_region, lambda operands: apply_block(operands[0], operands[1], operands[2], mpo_tensor, operands[3]), lambda operands: jnp.zeros(operands[0].shape, jnp.float32), (vector, left_one, right_one, offset_one))
            return lax.map(count_per_block, (vector_bf, left_part, right_part, offset_rows, live_mask))
        first = starting.astype(jnp.float32) * live_mask.astype(jnp.float32)[:, None, None, None]
        norm_sum = jnp.sum(first * first)
        inverse = lax.rsqrt(norm_sum + epsilon)
        current = first * inverse
        applied = operate(first.astype(jnp.bfloat16)) * inverse
        for iteration in range(DAV):
            quotient = jnp.sum(current * applied)
            residual = applied - quotient * current
            resid_sq = jnp.sum(residual * residual)
            factor = lax.rsqrt(resid_sq + epsilon)
            search = residual * factor
            probe_mapped_vector = operate(search.astype(jnp.bfloat16))
            curvature = jnp.sum(search * probe_mapped_vector)
            rotation = 0.5 * jnp.arctan2(-2.0 * resid_sq * factor, curvature - quotient)
            cos_part = jnp.cos(rotation)
            sin_part = jnp.sin(rotation)
            current = cos_part * current + sin_part * search
            applied = cos_part * applied + sin_part * probe_mapped_vector
        energy = jnp.sum(current * applied)
        state_out = (scale * current).astype(jnp.bfloat16)
        state_wide = state_out.astype(jnp.float32)
        density = jnp.einsum('nasb,ncsb->nac', state_wide, state_wide) / (PHYS * BLK)
        return (state_out, density, energy)
    state_out, density, energy = lax.map(region_solve, jnp.arange(LATTICE_PARTS, dtype=jnp.int32))
    return (state_out, density, energy)
```

```python
import math

import jax
import jax.numpy as jnp
import numpy as np
from jax import lax
from jax.experimental import pallas as pl
from jax.experimental.pallas import tpu as pltpu
from jax.sharding import PartitionSpec as P

DAV = 2
EPS = 1e-06
BLK = 128
PHYS = 4
CHAN = 16
ROWS = BLK * PHYS
GROUP = 4
STRIDE = 8

(NORM, SHIFT, RES, BACK, DIAG, DEEP, ON_F, ON_R, ON_D) = range(9)


def constants():
    lanes = np.zeros((4 * BLK, 4 * BLK), np.float32)
    for u in range(4):
        for a in range(BLK):
            lanes[u * BLK + a, (a // GROUP) * 16 + u * GROUP + a % GROUP] = 1.0
    rows = np.zeros((256, 64), np.float32)
    cols = np.zeros((64, 256), np.float32)
    same = np.zeros((256, 256), np.float32)
    for s in range(PHYS):
        for u in range(CHAN):
            for g in range(GROUP):
                rows[s * 64 + u * GROUP + g, u * PHYS + s] = 1.0
    for t in range(PHYS):
        for w in range(CHAN):
            for g in range(GROUP):
                cols[t * CHAN + w, w * 16 + g * PHYS + t] = 1.0
    index = np.arange(256)
    same[:, :] = (index[:, None] % GROUP) == ((index[None, :] // PHYS) % GROUP)
    return [jnp.asarray(m, jnp.bfloat16) for m in (lanes, rows, cols, same)]


def matmul(x, y):
    return jnp.dot(x, y, preferred_element_type=jnp.float32)


def total(x):
    return jnp.sum(jnp.sum(x, axis=0, keepdims=True), axis=1, keepdims=True)


def ratio(top, bottom):
    return jnp.where(bottom > 0.0, top / jnp.where(bottom > 0.0, bottom, 1.0), 0.0)


def krylov_kernel(
    live_ref, region_ref, start_ref, own_ref, left_ref, right_ref, mpo_ref, offset_ref,
    lanes_ref, rows_ref, cols_ref, same_ref,
    res_ref, deep_ref, sums_ref,
    operator, left_lanes, first_half, second_half, spread, shift, sums,
):
    slot = pl.program_id(0)

    @pl.when(slot == 0)
    def _():
        wide = matmul(rows_ref[...], mpo_ref[...]).astype(jnp.bfloat16)
        wide = matmul(wide, cols_ref[...]).astype(jnp.bfloat16)
        operator[...] = wide * same_ref[...]
        sums[...] = jnp.zeros_like(sums)

    def operate(vector):
        for pair in range(CHAN // 2):
            right = jnp.concatenate([right_ref[0, 2 * pair], right_ref[0, 2 * pair + 1]], axis=1)
            made = matmul(vector, right).astype(jnp.bfloat16)
            for j in range(2):
                w = 2 * pair + j
                for half in range(2):
                    part = made[half * 256:(half + 1) * 256, j * BLK:(j + 1) * BLK]
                    first_half[:, w * 16:(w + 1) * 16, half * BLK:(half + 1) * BLK] = part.reshape(16, 16, BLK)
        for g in range(16):
            made = matmul(operator[...], first_half[g]).astype(jnp.bfloat16)
            for half in range(2):
                for s in range(PHYS):
                    for ug in range(4):
                        at = ug * 512 + (half * 16 + g) * 16
                        second_half[at:at + 16, s * BLK:(s + 1) * BLK] = made[
                            s * 64 + ug * 16:s * 64 + ug * 16 + 16, half * BLK:(half + 1) * BLK]
        made = matmul(left_lanes[...], second_half[...])
        for s in range(PHYS):
            spread[pl.ds(s, BLK, stride=PHYS), :] = made[:, s * BLK:(s + 1) * BLK]
        return spread[...]

    def order_lanes(ref):
        for ug in range(4):
            four = jnp.concatenate([ref[0, 4 * ug + j] for j in range(4)], axis=1)
            left_lanes[:, ug * 512:(ug + 1) * 512] = matmul(four, lanes_ref[...]).astype(jnp.bfloat16)

    live = live_ref[0, 0]
    outer = region_ref[0] == 0

    @pl.when(jnp.logical_and(slot < live, outer))
    def _():
        order_lanes(own_ref)

    @pl.when(jnp.logical_and(slot < live, jnp.logical_not(outer)))
    def _():
        order_lanes(left_ref)

    @pl.when(slot < live)
    def _():
        column = jnp.broadcast_to(offset_ref[pl.ds(slot, 1), :], (BLK, BLK)).T
        for s in range(PHYS):
            shift[pl.ds(s, BLK, stride=PHYS), :] = column
        lane = lax.broadcasted_iota(jnp.int32, (1, BLK), 1)

        def note(quantity, value):
            sums[...] += jnp.where(lane == quantity * STRIDE + slot, value, 0.0)

        first = start_ref[0].astype(jnp.float32)
        image = operate(start_ref[0]) + shift[...] * first
        norm = total(first * first)
        quotient = ratio(total(first * image), norm)
        res = image - quotient * first
        res_ref[0] = res
        res_norm = total(res * res)
        note(NORM, norm)
        note(SHIFT, quotient)
        note(RES, res_norm)

        vector = res_ref[0].astype(jnp.bfloat16)
        image = operate(vector) + shift[...] * vector.astype(jnp.float32)
        first = start_ref[0].astype(jnp.float32)
        res = res_ref[0]
        back = ratio(total(first * image), norm)
        diag = ratio(total(res * image), res_norm)
        deep = image - back * first - diag * res
        deep_ref[0] = deep
        note(BACK, back)
        note(DIAG, diag)
        note(DEEP, total(deep * deep))

        vector = deep_ref[0].astype(jnp.bfloat16)
        image = operate(vector) + shift[...] * vector.astype(jnp.float32)
        note(ON_F, total(start_ref[0].astype(jnp.float32) * image))
        note(ON_R, total(res_ref[0] * image))
        note(ON_D, total(deep_ref[0] * image))

    sums_ref[...] = jnp.broadcast_to(sums[...], sums_ref.shape)


def rotate_kernel(
    scale, sectors, live_ref, all_ref, own_ref, start_ref, res_ref, deep_ref,
    state_ref, density_ref, energy_ref, spread,
):
    table = jnp.concatenate([all_ref[...], own_ref[...]], axis=0)
    shape = (sectors + own_ref.shape[0], BLK)
    row = lax.broadcasted_iota(jnp.int32, shape, 0)
    lane = lax.broadcasted_iota(jnp.int32, shape, 1)
    counted = jnp.logical_and(row < sectors, lane < STRIDE)

    def pick(quantity):
        return table if quantity == 0 else pltpu.roll(table, BLK - quantity * STRIDE, 1)

    def region_sum(x):
        return total(jnp.where(counted, x, 0.0))

    norm, shift, res_norm, back, diag, deep_norm, on_f, on_r, on_d = [pick(k) for k in range(9)]
    grams = (norm, res_norm, deep_norm)
    zero = jnp.zeros(shape, jnp.float32)

    def inner(x, y):
        made = x[0] * y[0] * grams[0]
        for k in (1, 2):
            made = made + x[k] * y[k] * grams[k]
        if len(y) > 3:
            made = made + y[3] * (x[0] * on_f + x[1] * on_r + x[2] * on_d)
        return region_sum(made)

    inverse = lax.rsqrt(region_sum(norm) + EPS)
    current = (zero + inverse, zero, zero)
    applied = (inverse * shift, zero + inverse, zero)
    for iteration in range(DAV):
        quotient = inner(current, applied)
        residual = tuple(x - quotient * y for x, y in zip(applied, current))
        resid_sq = inner(residual, residual)
        factor = lax.rsqrt(resid_sq + EPS)
        search = tuple(factor * x for x in residual)
        image = (search[0] * shift + search[1] * back, search[0] + search[1] * diag, search[1])
        if iteration == 1:
            image = image + (search[2],)
        curvature = inner(search, image)
        opposite = -2.0 * resid_sq * factor
        adjacent = curvature - quotient
        largest = jnp.maximum(jnp.abs(opposite), jnp.abs(adjacent))
        flat = largest == 0.0
        largest = jnp.where(flat, 1.0, largest)
        opposite = opposite / largest
        adjacent = jnp.where(flat, 1.0, adjacent / largest)
        length = jnp.sqrt(opposite * opposite + adjacent * adjacent)
        double_cos = jnp.abs(adjacent) / length
        double_sin = jnp.abs(opposite) / length
        large = jnp.sqrt(0.5 + 0.5 * double_cos)
        small = double_sin / (2.0 * large)
        ahead = adjacent >= 0.0
        cos_part = jnp.where(ahead, large, small)
        sin_part = -jnp.where(ahead, small, large)
        current = tuple(cos_part * x + sin_part * y for x, y in zip(current, search))
        turned = tuple(cos_part * x + sin_part * y for x, y in zip(applied, image))
        applied = turned + tuple(sin_part * y for y in image[3:])
    energy_ref[...] = jnp.broadcast_to(inner(current, applied), energy_ref.shape)
    mine = [scale * x[sectors:sectors + 1, :] for x in current]
    live = live_ref[0, 0]
    for slot in range(start_ref.shape[0]):

        @pl.when(slot < live)
        def _():
            on_first, on_res, on_deep = [x[:, slot:slot + 1] for x in mine]
            state = on_first * start_ref[slot].astype(jnp.float32)
            state = state + on_res * res_ref[slot] + on_deep * deep_ref[slot]
            state = state.astype(jnp.bfloat16)
            state_ref[slot] = state
            spread[...] = state.astype(jnp.float32)
            wide = jnp.concatenate(
                [spread[pl.ds(s, BLK, stride=PHYS), :] for s in range(PHYS)], axis=1
            ).astype(jnp.bfloat16)
            product = lax.dot_general(
                wide, wide, (((1,), (1,)), ((), ())), preferred_element_type=jnp.float32
            )
            density_ref[slot] = product * (1.0 / ROWS)

        @pl.when(slot >= live)
        def _():
            state_ref[slot] = jnp.zeros(state_ref.shape[1:], state_ref.dtype)
            density_ref[slot] = jnp.zeros(density_ref.shape[1:], density_ref.dtype)


def from_behind(shard, axis, by):
    length = lax.axis_size(axis)
    return lax.ppermute(shard, axis, [(i, i + by) for i in range(length - by)])


def entering(decay, terms, axis):
    pair = from_behind(jnp.stack([decay, terms]), axis, 1)
    by = 1
    while by < lax.axis_size(axis):
        earlier = from_behind(pair, axis, by)
        pair = jnp.stack([pair[0] * earlier[0], pair[0] * earlier[1] + pair[1]])
        by *= 2
    return pair[1]


def body(start_state, left_env, right_env, mpo_tensor, decay, energy_terms, live_count):
    slots = start_state.shape[1]
    sectors = lax.axis_size("sector")
    start = start_state.reshape(slots, ROWS, BLK)
    arrived = from_behind(left_env[0], "region", 1)
    offsets = entering(decay[0], energy_terms[0], "region")
    region = lax.axis_index("region").reshape(1).astype(jnp.int32)
    mpo = mpo_tensor.reshape(CHAN * PHYS, PHYS * CHAN)

    def block(*shape):
        return pl.BlockSpec((1,) + shape, lambda n: (n,) + (0,) * len(shape))

    def whole(*shape):
        return pl.BlockSpec(shape, lambda n: (0,) * len(shape))

    smem = pl.BlockSpec(memory_space=pltpu.SMEM)
    res, deep, sums = pl.pallas_call(
        krylov_kernel,
        grid=(slots,),
        in_specs=[
            smem, smem, block(ROWS, BLK), block(CHAN, BLK, BLK), block(CHAN, BLK, BLK),
            block(CHAN, BLK, BLK), whole(64, 64), whole(slots, BLK),
            whole(512, 512), whole(256, 64), whole(64, 256), whole(256, 256),
        ],
        out_specs=[block(ROWS, BLK), block(ROWS, BLK), whole(sectors, BLK)],
        out_shape=[
            jax.ShapeDtypeStruct((slots, ROWS, BLK), jnp.float32),
            jax.ShapeDtypeStruct((slots, ROWS, BLK), jnp.float32),
            jax.ShapeDtypeStruct((sectors, BLK), jnp.float32),
        ],
        scratch_shapes=[
            pltpu.VMEM((256, 256), jnp.bfloat16),
            pltpu.VMEM((BLK, CHAN * BLK), jnp.bfloat16),
            pltpu.VMEM((16, 256, 256), jnp.bfloat16),
            pltpu.VMEM((CHAN * BLK, ROWS), jnp.bfloat16),
            pltpu.VMEM((ROWS, BLK), jnp.float32),
            pltpu.VMEM((ROWS, BLK), jnp.float32),
            pltpu.VMEM((1, BLK), jnp.float32),
        ],
        compiler_params=pltpu.CompilerParams(vmem_limit_bytes=40 << 20),
        name="krylov",
    )(live_count, region, start, left_env[0], arrived, right_env[0], mpo, offsets, *constants())
    every = lax.all_to_all(sums.reshape(sectors, 1, BLK), "sector", 0, 0).reshape(sectors, BLK)
    vmem = pl.BlockSpec(memory_space=pltpu.VMEM)
    state, density, energy = pl.pallas_call(
        lambda *refs: rotate_kernel(math.sqrt(slots * sectors * ROWS * BLK), sectors, *refs),
        in_specs=[smem] + [vmem] * 5,
        out_specs=[vmem] * 3,
        out_shape=[
            jax.ShapeDtypeStruct((slots, ROWS, BLK), jnp.bfloat16),
            jax.ShapeDtypeStruct((slots, BLK, BLK), jnp.float32),
            jax.ShapeDtypeStruct((1, 1), jnp.float32),
        ],
        scratch_shapes=[pltpu.VMEM((ROWS, BLK), jnp.float32)],
        compiler_params=pltpu.CompilerParams(vmem_limit_bytes=24 << 20),
        name="rotate",
    )(live_count, every, sums[:8], start, res, deep)
    return (state.reshape(start_state.shape), density[None], energy.reshape(1))


def solution(mesh):
    in_specs = (
        P("region", "sector", None, None, None),
        P("region", "sector", None, None, None),
        P("region", "sector", None, None, None),
        P(),
        P("region", "sector", None),
        P("region", "sector", None),
        P("region", "sector"),
    )
    out_specs = (
        P("region", "sector", None, None, None),
        P("region", "sector", None, None),
        P("region"),
    )
    return jax.shard_map(body, mesh=mesh, in_specs=in_specs, out_specs=out_specs, check_vma=False)
```

```python
import functools
import math

import jax
import jax.numpy as jnp
import numpy as np
from jax import lax
from jax.experimental import pallas as pl
from jax.experimental.pallas import tpu as pltpu
from jax.sharding import PartitionSpec as P

DAV = 2
EPS = 1e-06
BLK = 128
PHYS = 4
CHAN = 16
ROWS = BLK * PHYS
GROUP = 4
VMEM_LIMIT = 56 << 20
GROUPED = 2
STRIDE = 8

(NORM, SHIFT, RES, BACK, DIAG, DEEP, ON_F, ON_R, ON_D) = range(9)


def constants():
    lanes = np.zeros((4 * BLK, 4 * BLK), np.float32)
    for u in range(4):
        for a in range(BLK):
            lanes[u * BLK + a, (a // GROUP) * 16 + u * GROUP + a % GROUP] = 1.0
    rows = np.zeros((256, 64), np.float32)
    cols = np.zeros((64, 256), np.float32)
    same = np.zeros((256, 256), np.float32)
    for s in range(PHYS):
        for u in range(CHAN):
            for g in range(GROUP):
                rows[s * 64 + u * GROUP + g, u * PHYS + s] = 1.0
    for t in range(PHYS):
        for w in range(CHAN):
            for g in range(GROUP):
                cols[t * CHAN + w, w * 16 + g * PHYS + t] = 1.0
    index = np.arange(256)
    same[:, :] = (index[:, None] % GROUP) == ((index[None, :] // PHYS) % GROUP)
    return [jnp.asarray(m, jnp.bfloat16) for m in (lanes, rows, cols, same)]


def matmul(x, y):
    return jnp.dot(x, y, preferred_element_type=jnp.float32)


def total(x):
    return jnp.sum(jnp.sum(x, axis=0, keepdims=True), axis=1, keepdims=True)


def ratio(top, bottom):
    return jnp.where(bottom > 0.0, top / jnp.where(bottom > 0.0, bottom, 1.0), 0.0)


def operator_kernel(mpo_ref, rows_ref, cols_ref, same_ref, operator_ref):
    wide = matmul(rows_ref[...], mpo_ref[...]).astype(jnp.bfloat16)
    wide = matmul(wide, cols_ref[...]).astype(jnp.bfloat16)
    operator_ref[...] = wide * same_ref[...]


def krylov_kernel(
    base, live_ref, region_ref, before_ref, offset_ref, operator_ref,
    start_hbm, own_hbm, left_hbm, right_hbm, lanes_hbm,
    sums_ref, res_hbm, deep_hbm,
    start_ref, left_ref, right_ref, lanes_ref, res_ref, deep_ref,
    left_lanes, first_half, second_half, spread, shift, sems,
):
    group = range(start_ref.shape[0])

    def operate_right(i, vector):
        for pair in range(CHAN // 2):
            right = jnp.concatenate([right_ref[i, 2 * pair], right_ref[i, 2 * pair + 1]], axis=1)
            made = matmul(vector, right).astype(jnp.bfloat16)
            for j in range(2):
                w = 2 * pair + j
                for half in range(2):
                    part = made[half * 256:(half + 1) * 256, j * BLK:(j + 1) * BLK]
                    first_half[i, :, w * 16:(w + 1) * 16, half * BLK:(half + 1) * BLK] = part.reshape(16, 16, BLK)
        for g in range(16):
            made = matmul(operator_ref[...], first_half[i, g]).astype(jnp.bfloat16)
            for half in range(2):
                for s in range(PHYS):
                    for ug in range(4):
                        at = ug * 512 + (half * 16 + g) * 16
                        second_half[i, at:at + 16, s * BLK:(s + 1) * BLK] = made[
                            s * 64 + ug * 16:s * 64 + ug * 16 + 16, half * BLK:(half + 1) * BLK]

    def operate_left(i):
        made = matmul(left_lanes[i], second_half[i])
        for s in range(PHYS):
            spread[i, pl.ds(s, BLK, stride=PHYS), :] = made[:, s * BLK:(s + 1) * BLK]
        return spread[i]

    def order_lanes(i):
        for ug in range(4):
            four = jnp.concatenate([left_ref[i, 4 * ug + j] for j in range(4)], axis=1)
            left_lanes[i, :, ug * 512:(ug + 1) * 512] = matmul(four, lanes_ref[...]).astype(jnp.bfloat16)

    live = live_ref[0, 0]
    outer = region_ref[0] == 0
    lane = lax.broadcasted_iota(jnp.int32, (1, BLK), 1)

    @pl.when(base < live)
    def _():
        start_in = pltpu.make_async_copy(start_hbm.at[pl.ds(base, len(group))], start_ref, sems.at[0])
        right_in = [
            pltpu.make_async_copy(right_hbm.at[base + i], right_ref.at[i], sems.at[6 + i]) for i in group
        ]
        lanes_in = pltpu.make_async_copy(lanes_hbm, lanes_ref, sems.at[2])
        left_in = pltpu.make_async_copy(left_hbm, left_ref, sems.at[3])
        start_in.start()
        right_in[0].start()
        lanes_in.start()

        @pl.when(outer)
        def _():
            pltpu.make_async_copy(own_hbm.at[pl.ds(base, len(group))], left_ref, sems.at[3]).start()

        @pl.when(jnp.logical_not(outer))
        def _():
            left_in.start()

        for copy in right_in[1:]:
            copy.start()
        sums = before_ref[...]

        def note(sums, i, quantity, value):
            slot = base + i
            return sums + jnp.where(jnp.logical_and(lane == quantity * STRIDE + slot, slot < live), value, 0.0)

        for i in group:
            column = jnp.broadcast_to(offset_ref[base + i:base + i + 1, :], (BLK, BLK)).T
            for s in range(PHYS):
                shift[i, pl.ds(s, BLK, stride=PHYS), :] = column
        start_in.wait()
        for i in group:
            right_in[i].wait()
        lanes_in.wait()
        left_in.wait()
        res_out = pltpu.make_async_copy(res_ref, res_hbm, sems.at[4])
        deep_out = pltpu.make_async_copy(deep_ref, deep_hbm, sems.at[5])
        norm, res_norm = {}, {}

        for i in group:
            operate_right(i, start_ref[i])
            order_lanes(i)
        for i in group:
            first = start_ref[i].astype(jnp.float32)
            image = operate_left(i) + shift[i] * first
            norm[i] = total(first * first)
            quotient = ratio(total(first * image), norm[i])
            res = image - quotient * first
            res_ref[i] = res
            res_norm[i] = total(res * res)
            sums = note(note(note(sums, i, NORM, norm[i]), i, SHIFT, quotient), i, RES, res_norm[i])

        for i in group:
            operate_right(i, res_ref[i].astype(jnp.bfloat16))
        for i in group:
            res = res_ref[i]
            first = start_ref[i].astype(jnp.float32)
            image = operate_left(i) + shift[i] * res.astype(jnp.bfloat16).astype(jnp.float32)
            back = ratio(total(first * image), norm[i])
            diag = ratio(total(res * image), res_norm[i])
            deep = image - back * first - diag * res
            deep_ref[i] = deep
            sums = note(note(note(sums, i, BACK, back), i, DIAG, diag), i, DEEP, total(deep * deep))

        for i in group:
            operate_right(i, deep_ref[i].astype(jnp.bfloat16))
        for i in group:
            deep = deep_ref[i]
            image = operate_left(i) + shift[i] * deep.astype(jnp.bfloat16).astype(jnp.float32)
            sums = note(sums, i, ON_F, total(start_ref[i].astype(jnp.float32) * image))
            sums = note(sums, i, ON_R, total(res_ref[i] * image))
            sums = note(sums, i, ON_D, total(deep * image))
        res_out.start()
        deep_out.start()
        sums_ref[...] = jnp.broadcast_to(sums, sums_ref.shape)
        res_out.wait()
        deep_out.wait()

    @pl.when(base >= live)
    def _():
        sums_ref[...] = jnp.broadcast_to(before_ref[...], sums_ref.shape)


def rotate_kernel(
    scale, slots, sectors, live_ref, all_ref, own_ref, start_hbm, *refs
):
    groups = slots // GROUPED
    res_hbm, deep_hbm = refs[:groups], refs[groups:2 * groups]
    state_hbm, density_hbm, energy_ref = refs[2 * groups:2 * groups + 3]
    start_ref, res_ref, deep_ref, state_ref, density_ref, spread, sems = refs[2 * groups + 3:]
    live = live_ref[0, 0]

    def coming(slot):
        return (
            pltpu.make_async_copy(start_hbm.at[slot], start_ref.at[slot], sems.at[0, slot]),
            pltpu.make_async_copy(res_hbm[slot // GROUPED].at[slot % GROUPED], res_ref.at[slot], sems.at[1, slot]),
            pltpu.make_async_copy(deep_hbm[slot // GROUPED].at[slot % GROUPED], deep_ref.at[slot], sems.at[2, slot]),
        )

    def going(slot):
        return (
            pltpu.make_async_copy(state_ref.at[slot], state_hbm.at[slot], sems.at[3, slot]),
            pltpu.make_async_copy(density_ref.at[slot], density_hbm.at[slot], sems.at[4, slot]),
        )

    for slot in range(slots):

        @pl.when(slot < live)
        def _():
            for copy in coming(slot):
                copy.start()

        @pl.when(slot >= live)
        def _():
            state_ref[slot] = jnp.zeros(state_ref.shape[1:], state_ref.dtype)
            density_ref[slot] = jnp.zeros(density_ref.shape[1:], density_ref.dtype)
            for copy in going(slot):
                copy.start()

    table = jnp.concatenate([all_ref[...], own_ref[0:8, :]], axis=0)
    shape = (sectors + 8, BLK)
    row = lax.broadcasted_iota(jnp.int32, shape, 0)
    lane = lax.broadcasted_iota(jnp.int32, shape, 1)
    counted = jnp.logical_and(row < sectors, lane < STRIDE)

    def pick(quantity):
        return table if quantity == 0 else pltpu.roll(table, BLK - quantity * STRIDE, 1)

    def region_sum(x):
        return total(jnp.where(counted, x, 0.0))

    norm, shift, res_norm, back, diag, deep_norm, on_f, on_r, on_d = [pick(k) for k in range(9)]
    grams = (norm, res_norm, deep_norm)
    zero = jnp.zeros(shape, jnp.float32)

    def inner(x, y):
        made = x[0] * y[0] * grams[0]
        for k in (1, 2):
            made = made + x[k] * y[k] * grams[k]
        if len(y) > 3:
            made = made + y[3] * (x[0] * on_f + x[1] * on_r + x[2] * on_d)
        return region_sum(made)

    inverse = lax.rsqrt(region_sum(norm) + EPS)
    current = (zero + inverse, zero, zero)
    applied = (inverse * shift, zero + inverse, zero)
    for iteration in range(DAV):
        quotient = inner(current, applied)
        residual = tuple(x - quotient * y for x, y in zip(applied, current))
        resid_sq = inner(residual, residual)
        factor = lax.rsqrt(resid_sq + EPS)
        search = tuple(factor * x for x in residual)
        image = (search[0] * shift + search[1] * back, search[0] + search[1] * diag, search[1])
        if iteration == 1:
            image = image + (search[2],)
        curvature = inner(search, image)
        opposite = -2.0 * resid_sq * factor
        adjacent = curvature - quotient
        largest = jnp.maximum(jnp.abs(opposite), jnp.abs(adjacent))
        flat = largest == 0.0
        largest = jnp.where(flat, 1.0, largest)
        opposite = opposite / largest
        adjacent = jnp.where(flat, 1.0, adjacent / largest)
        length = jnp.sqrt(opposite * opposite + adjacent * adjacent)
        double_cos = jnp.abs(adjacent) / length
        double_sin = jnp.abs(opposite) / length
        large = jnp.sqrt(0.5 + 0.5 * double_cos)
        small = double_sin / (2.0 * large)
        ahead = adjacent >= 0.0
        cos_part = jnp.where(ahead, large, small)
        sin_part = -jnp.where(ahead, small, large)
        current = tuple(cos_part * x + sin_part * y for x, y in zip(current, search))
        turned = tuple(cos_part * x + sin_part * y for x, y in zip(applied, image))
        applied = turned + tuple(sin_part * y for y in image[3:])
    energy_ref[...] = jnp.broadcast_to(inner(current, applied), energy_ref.shape)
    mine = [scale * x[sectors:sectors + 1, :] for x in current]
    for slot in range(slots):

        @pl.when(slot < live)
        def _():
            for copy in coming(slot):
                copy.wait()
            on_first, on_res, on_deep = [x[:, slot:slot + 1] for x in mine]
            state = on_first * start_ref[slot].astype(jnp.float32)
            state = state + on_res * res_ref[slot] + on_deep * deep_ref[slot]
            state = state.astype(jnp.bfloat16)
            state_ref[slot] = state
            spread[slot] = state.astype(jnp.float32)
            wide = jnp.concatenate(
                [spread[slot, pl.ds(s, BLK, stride=PHYS), :] for s in range(PHYS)], axis=1
            ).astype(jnp.bfloat16)
            product = lax.dot_general(
                wide, wide, (((1,), (1,)), ((), ())), preferred_element_type=jnp.float32
            )
            density_ref[slot] = product * (1.0 / ROWS)
            for copy in going(slot):
                copy.start()

    for slot in range(slots):
        for copy in going(slot):
            copy.wait()


def from_behind(shard, axis, by):
    length = lax.axis_size(axis)
    return lax.ppermute(shard, axis, [(i, i + by) for i in range(length - by)])


def entering(decay, terms, axis):
    slots = decay.shape[0]
    own = jnp.concatenate([decay, terms], axis=0)
    other = lax.ppermute(own, axis, [(i, i ^ 1) for i in range(lax.axis_size(axis))])
    second = lax.axis_index(axis) % 2 == 1
    early, late = jnp.where(second, other, own), jnp.where(second, own, other)
    pair = jnp.concatenate(
        [early[:slots] * late[:slots], late[:slots] * early[slots:] + late[slots:]], axis=0
    )
    total = jnp.zeros_like(terms)
    for by in (6, 4, 2):
        earlier = from_behind(pair, axis, by)
        total = earlier[:slots] * total + earlier[slots:]
    return jnp.where(second, early[:slots] * total + early[slots:], total)


def body(start_state, left_env, right_env, mpo_tensor, decay, energy_terms, live_count):
    slots = start_state.shape[1]
    sectors = lax.axis_size("sector")
    start = start_state.reshape(slots, ROWS, BLK)
    offsets = entering(decay[0], energy_terms[0], "region")
    arrived = [from_behind(left_env[0, at:at + GROUPED], "region", 1) for at in range(0, slots, GROUPED)]
    region = lax.axis_index("region").reshape(1).astype(jnp.int32)
    mpo = mpo_tensor.reshape(CHAN * PHYS, PHYS * CHAN)
    lanes, rows, cols, same = constants()

    smem = pl.BlockSpec(memory_space=pltpu.SMEM)
    vmem = pl.BlockSpec(memory_space=pltpu.VMEM)
    hbm = pl.BlockSpec(memory_space=pl.ANY)
    vectors = jax.ShapeDtypeStruct((GROUPED, ROWS, BLK), jnp.float32)
    operator = pl.pallas_call(
        operator_kernel,
        in_specs=[vmem] * 4,
        out_specs=vmem,
        out_shape=jax.ShapeDtypeStruct((256, 256), jnp.bfloat16),
        name="operator",
    )(mpo, rows, cols, same)
    sums = jnp.zeros((1, BLK), jnp.float32)
    res, deep = [], []
    for base in range(0, slots, GROUPED):
        copies = sectors if base + GROUPED == slots else 1
        sums, res_one, deep_one = pl.pallas_call(
            functools.partial(krylov_kernel, base),
            in_specs=[smem, smem, vmem, vmem, vmem, hbm, hbm, hbm, hbm, hbm],
            out_specs=[vmem, hbm, hbm],
            out_shape=[jax.ShapeDtypeStruct((copies, BLK), jnp.float32), vectors, vectors],
            scratch_shapes=[
                pltpu.VMEM((GROUPED, ROWS, BLK), jnp.bfloat16),
                pltpu.VMEM((GROUPED, CHAN, BLK, BLK), jnp.bfloat16),
                pltpu.VMEM((GROUPED, CHAN, BLK, BLK), jnp.bfloat16),
                pltpu.VMEM((4 * BLK, 4 * BLK), jnp.bfloat16),
                pltpu.VMEM((GROUPED, ROWS, BLK), jnp.float32),
                pltpu.VMEM((GROUPED, ROWS, BLK), jnp.float32),
                pltpu.VMEM((GROUPED, BLK, CHAN * BLK), jnp.bfloat16),
                pltpu.VMEM((GROUPED, 16, 256, 256), jnp.bfloat16),
                pltpu.VMEM((GROUPED, CHAN * BLK, ROWS), jnp.bfloat16),
                pltpu.VMEM((GROUPED, ROWS, BLK), jnp.float32),
                pltpu.VMEM((GROUPED, ROWS, BLK), jnp.float32),
                pltpu.SemaphoreType.DMA((6 + GROUPED,)),
            ],
            compiler_params=pltpu.CompilerParams(vmem_limit_bytes=VMEM_LIMIT),
            cost_estimate=pl.CostEstimate(flops=10**10, bytes_accessed=1 << 22, transcendentals=0),
            name="krylov",
        )(
            live_count, region, sums, offsets, operator,
            start, left_env[0], arrived[base // GROUPED], right_env[0], lanes,
        )
        res.append(res_one)
        deep.append(deep_one)
    every = lax.all_to_all(sums.reshape(sectors, 1, BLK), "sector", 0, 0).reshape(sectors, BLK)
    state, density, energy = pl.pallas_call(
        functools.partial(rotate_kernel, math.sqrt(slots * sectors * ROWS * BLK), slots, sectors),
        in_specs=[smem, vmem, vmem] + [hbm] * (1 + 2 * (slots // GROUPED)),
        out_specs=[hbm, hbm, vmem],
        out_shape=[
            jax.ShapeDtypeStruct((slots, ROWS, BLK), jnp.bfloat16),
            jax.ShapeDtypeStruct((slots, BLK, BLK), jnp.float32),
            jax.ShapeDtypeStruct((1, 1), jnp.float32),
        ],
        scratch_shapes=[
            pltpu.VMEM((slots, ROWS, BLK), jnp.bfloat16),
            pltpu.VMEM((slots, ROWS, BLK), jnp.float32),
            pltpu.VMEM((slots, ROWS, BLK), jnp.float32),
            pltpu.VMEM((slots, ROWS, BLK), jnp.bfloat16),
            pltpu.VMEM((slots, BLK, BLK), jnp.float32),
            pltpu.VMEM((slots, ROWS, BLK), jnp.float32),
            pltpu.SemaphoreType.DMA((5, slots)),
        ],
        compiler_params=pltpu.CompilerParams(vmem_limit_bytes=VMEM_LIMIT),
        name="rotate",
    )(live_count, every, sums, start, *res, *deep)
    return (state.reshape(start_state.shape), density[None], energy.reshape(1))


def solution(mesh):
    in_specs = (
        P("region", "sector", None, None, None),
        P("region", "sector", None, None, None),
        P("region", "sector", None, None, None),
        P(),
        P("region", "sector", None),
        P("region", "sector", None),
        P("region", "sector"),
    )
    out_specs = (
        P("region", "sector", None, None, None),
        P("region", "sector", None, None),
        P("region"),
    )
    return jax.shard_map(body, mesh=mesh, in_specs=in_specs, out_specs=out_specs, check_vma=False)
```

```python
import functools
import math

import jax
import jax.numpy as jnp
import numpy as np
from jax import lax
from jax.experimental import pallas as pl
from jax.experimental.pallas import tpu as pltpu
from jax.sharding import PartitionSpec as P

DAV = 2
EPS = 1e-06
BLK = 128
PHYS = 4
CHAN = 16
ROWS = BLK * PHYS
GROUP = 4
VMEM_LIMIT = 56 << 20
GROUPED = 2
STRIDE = 8

(NORM, SHIFT, RES, BACK, DIAG, DEEP, ON_F, ON_R, ON_D) = range(9)


def constants():
    lanes = np.zeros((4 * BLK, 4 * BLK), np.float32)
    for u in range(4):
        for a in range(BLK):
            lanes[u * BLK + a, (a // GROUP) * 16 + u * GROUP + a % GROUP] = 1.0
    rows = np.zeros((256, 64), np.float32)
    cols = np.zeros((64, 256), np.float32)
    same = np.zeros((256, 256), np.float32)
    for s in range(PHYS):
        for u in range(CHAN):
            for g in range(GROUP):
                rows[s * 64 + u * GROUP + g, u * PHYS + s] = 1.0
    for t in range(PHYS):
        for w in range(CHAN):
            for g in range(GROUP):
                cols[t * CHAN + w, w * 16 + g * PHYS + t] = 1.0
    index = np.arange(256)
    same[:, :] = (index[:, None] % GROUP) == ((index[None, :] // PHYS) % GROUP)
    return [jnp.asarray(m, jnp.bfloat16) for m in (lanes, rows, cols, same)]


def matmul(x, y):
    return jnp.dot(x, y, preferred_element_type=jnp.float32)


def total(x):
    return jnp.sum(jnp.sum(x, axis=0, keepdims=True), axis=1, keepdims=True)


def ratio(top, bottom):
    return jnp.where(bottom > 0.0, top / jnp.where(bottom > 0.0, bottom, 1.0), 0.0)


def krylov_kernel(
    base, live_ref, region_ref, offset_hbm, start_hbm, own_hbm, left_hbm, right_hbm, lanes_hbm, *refs
):
    head = base == 0
    if head:
        small_hbm, (sums_ref, res_hbm, deep_hbm, operator_hbm) = refs[:4], refs[4:8]
        refs = refs[8:]
    else:
        small_hbm, (sums_ref, res_hbm, deep_hbm) = refs[:2], refs[2:5]
        refs = refs[5:]
    (
        start_ref, left_ref, right_ref, lanes_ref, res_ref, deep_ref,
        left_lanes, first_half, second_half, spread, shift, offset_ref, operator_ref, sems, *small,
    ) = refs
    if not head:
        small = [operator_ref] + small
    group = range(start_ref.shape[0])

    def operate_right(i, vector):
        for pair in range(CHAN // 2):
            right = jnp.concatenate([right_ref[i, 2 * pair], right_ref[i, 2 * pair + 1]], axis=1)
            made = matmul(vector, right).astype(jnp.bfloat16)
            for j in range(2):
                w = 2 * pair + j
                for half in range(2):
                    part = made[half * 256:(half + 1) * 256, j * BLK:(j + 1) * BLK]
                    first_half[i, :, w * 16:(w + 1) * 16, half * BLK:(half + 1) * BLK] = part.reshape(16, 16, BLK)
        for g in range(16):
            made = matmul(operator_ref[...], first_half[i, g]).astype(jnp.bfloat16)
            for half in range(2):
                for s in range(PHYS):
                    for ug in range(4):
                        at = ug * 512 + (half * 16 + g) * 16
                        second_half[i, at:at + 16, s * BLK:(s + 1) * BLK] = made[
                            s * 64 + ug * 16:s * 64 + ug * 16 + 16, half * BLK:(half + 1) * BLK]

    def operate_left(i):
        made = matmul(left_lanes[i], second_half[i])
        for s in range(PHYS):
            spread[i, pl.ds(s, BLK, stride=PHYS), :] = made[:, s * BLK:(s + 1) * BLK]
        return spread[i]

    def order_lanes(i):
        for ug in range(4):
            four = jnp.concatenate([left_ref[i, 4 * ug + j] for j in range(4)], axis=1)
            left_lanes[i, :, ug * 512:(ug + 1) * 512] = matmul(four, lanes_ref[...]).astype(jnp.bfloat16)

    live = live_ref[0, 0]
    outer = region_ref[0] == 0
    lane = lax.broadcasted_iota(jnp.int32, (1, BLK), 1)

    @pl.when(base < live)
    def _():
        start_in = pltpu.make_async_copy(start_hbm.at[pl.ds(base, len(group))], start_ref, sems.at[0])
        right_in = [
            pltpu.make_async_copy(right_hbm.at[base + i], right_ref.at[i], sems.at[6 + i]) for i in group
        ]
        lanes_in = pltpu.make_async_copy(lanes_hbm, lanes_ref, sems.at[2])
        left_in = pltpu.make_async_copy(left_hbm, left_ref, sems.at[3])
        small_in = [
            pltpu.make_async_copy(hbm, ref, sems.at[6 + len(group) + k])
            for k, (hbm, ref) in enumerate(zip([offset_hbm] + list(small_hbm), [offset_ref] + small))
        ]
        for copy in small_in:
            copy.start()
        start_in.start()
        for copy in right_in:
            copy.start()
        lanes_in.start()

        @pl.when(outer)
        def _():
            pltpu.make_async_copy(own_hbm.at[pl.ds(base, len(group))], left_ref, sems.at[3]).start()

        @pl.when(jnp.logical_not(outer))
        def _():
            left_in.start()

        for copy in small_in:
            copy.wait()
        if head:
            mpo_ref, rows_ref, cols_ref, same_ref = small
            sums = jnp.zeros((1, BLK), jnp.float32)
            wide = matmul(rows_ref[...], mpo_ref[...]).astype(jnp.bfloat16)
            wide = matmul(wide, cols_ref[...]).astype(jnp.bfloat16)
            operator_ref[...] = wide * same_ref[...]
            operator_out = pltpu.make_async_copy(operator_ref, operator_hbm, sems.at[6 + len(group) + 5])
            operator_out.start()
        else:
            sums = small[1][...]

        def note(sums, i, quantity, value):
            slot = base + i
            return sums + jnp.where(jnp.logical_and(lane == quantity * STRIDE + slot, slot < live), value, 0.0)

        for i in group:
            column = jnp.broadcast_to(offset_ref[base + i:base + i + 1, :], (BLK, BLK)).T
            for s in range(PHYS):
                shift[i, pl.ds(s, BLK, stride=PHYS), :] = column
        res_out = pltpu.make_async_copy(res_ref, res_hbm, sems.at[4])
        deep_out = pltpu.make_async_copy(deep_ref, deep_hbm, sems.at[5])
        norm, res_norm = {}, {}

        start_in.wait()
        for i in group:
            right_in[i].wait()
            operate_right(i, start_ref[i])
        lanes_in.wait()
        left_in.wait()
        for i in group:
            order_lanes(i)
        for i in group:
            first = start_ref[i].astype(jnp.float32)
            image = operate_left(i) + shift[i] * first
            norm[i] = total(first * first)
            quotient = ratio(total(first * image), norm[i])
            res = image - quotient * first
            res_ref[i] = res
            res_norm[i] = total(res * res)
            sums = note(note(note(sums, i, NORM, norm[i]), i, SHIFT, quotient), i, RES, res_norm[i])

        res_out.start()
        for i in group:
            operate_right(i, res_ref[i].astype(jnp.bfloat16))
        for i in group:
            res = res_ref[i]
            first = start_ref[i].astype(jnp.float32)
            image = operate_left(i) + shift[i] * res.astype(jnp.bfloat16).astype(jnp.float32)
            back = ratio(total(first * image), norm[i])
            diag = ratio(total(res * image), res_norm[i])
            deep = image - back * first - diag * res
            deep_ref[i] = deep
            sums = note(note(note(sums, i, BACK, back), i, DIAG, diag), i, DEEP, total(deep * deep))

        deep_out.start()
        for i in group:
            operate_right(i, deep_ref[i].astype(jnp.bfloat16))
        for i in group:
            deep = deep_ref[i]
            image = operate_left(i) + shift[i] * deep.astype(jnp.bfloat16).astype(jnp.float32)
            sums = note(sums, i, ON_F, total(start_ref[i].astype(jnp.float32) * image))
            sums = note(sums, i, ON_R, total(res_ref[i] * image))
            sums = note(sums, i, ON_D, total(deep * image))
        sums_ref[...] = jnp.broadcast_to(sums, sums_ref.shape)
        res_out.wait()
        deep_out.wait()
        if head:
            operator_out.wait()

    if not head:

        @pl.when(base >= live)
        def _():
            before_in = pltpu.make_async_copy(small_hbm[1], small[1], sems.at[0])
            before_in.start()
            before_in.wait()
            sums_ref[...] = jnp.broadcast_to(small[1][...], sums_ref.shape)


def rotate_kernel(
    scale, slots, sectors, live_ref, all_hbm, own_hbm, start_hbm, *refs
):
    groups = slots // GROUPED
    res_hbm, deep_hbm = refs[:groups], refs[groups:2 * groups]
    state_hbm, density_hbm, energy_ref = refs[2 * groups:2 * groups + 3]
    table_ref, start_ref, res_ref, deep_ref, state_ref, density_ref, spread, sems = refs[2 * groups + 3:]
    live = live_ref[0, 0]
    tables = [
        pltpu.make_async_copy(all_hbm, table_ref.at[pl.ds(0, sectors)], sems.at[0, 0]),
        pltpu.make_async_copy(own_hbm.at[pl.ds(0, 8)], table_ref.at[pl.ds(sectors, 8)], sems.at[1, 0]),
    ]
    coming = [pltpu.make_async_copy(start_hbm, start_ref, sems.at[2, 0])]
    for group in range(groups):
        rows = pl.ds(group * GROUPED, GROUPED)
        coming.append(pltpu.make_async_copy(res_hbm[group], res_ref.at[rows], sems.at[0, 1 + group]))
        coming.append(pltpu.make_async_copy(deep_hbm[group], deep_ref.at[rows], sems.at[1, 1 + group]))
    for copy in tables + coming:
        copy.start()
    for copy in tables:
        copy.wait()
    table = table_ref[...]
    shape = (sectors + 8, BLK)
    row = lax.broadcasted_iota(jnp.int32, shape, 0)
    lane = lax.broadcasted_iota(jnp.int32, shape, 1)
    counted = jnp.logical_and(row < sectors, lane < STRIDE)

    def pick(quantity):
        return table if quantity == 0 else pltpu.roll(table, BLK - quantity * STRIDE, 1)

    def region_sum(x):
        return total(jnp.where(counted, x, 0.0))

    norm, shift, res_norm, back, diag, deep_norm, on_f, on_r, on_d = [pick(k) for k in range(9)]
    grams = (norm, res_norm, deep_norm)
    zero = jnp.zeros(shape, jnp.float32)

    def inner(x, y):
        made = x[0] * y[0] * grams[0]
        for k in (1, 2):
            made = made + x[k] * y[k] * grams[k]
        if len(y) > 3:
            made = made + y[3] * (x[0] * on_f + x[1] * on_r + x[2] * on_d)
        return region_sum(made)

    inverse = lax.rsqrt(region_sum(norm) + EPS)
    current = (zero + inverse, zero, zero)
    applied = (inverse * shift, zero + inverse, zero)
    for iteration in range(DAV):
        quotient = inner(current, applied)
        residual = tuple(x - quotient * y for x, y in zip(applied, current))
        resid_sq = inner(residual, residual)
        factor = lax.rsqrt(resid_sq + EPS)
        search = tuple(factor * x for x in residual)
        image = (search[0] * shift + search[1] * back, search[0] + search[1] * diag, search[1])
        if iteration == 1:
            image = image + (search[2],)
        curvature = inner(search, image)
        opposite = -2.0 * resid_sq * factor
        adjacent = curvature - quotient
        largest = jnp.maximum(jnp.abs(opposite), jnp.abs(adjacent))
        flat = largest == 0.0
        largest = jnp.where(flat, 1.0, largest)
        opposite = opposite / largest
        adjacent = jnp.where(flat, 1.0, adjacent / largest)
        length = jnp.sqrt(opposite * opposite + adjacent * adjacent)
        double_cos = jnp.abs(adjacent) / length
        double_sin = jnp.abs(opposite) / length
        large = jnp.sqrt(0.5 + 0.5 * double_cos)
        small = double_sin / (2.0 * large)
        ahead = adjacent >= 0.0
        cos_part = jnp.where(ahead, large, small)
        sin_part = -jnp.where(ahead, small, large)
        current = tuple(cos_part * x + sin_part * y for x, y in zip(current, search))
        turned = tuple(cos_part * x + sin_part * y for x, y in zip(applied, image))
        applied = turned + tuple(sin_part * y for y in image[3:])
    energy_ref[...] = jnp.broadcast_to(inner(current, applied), energy_ref.shape)
    mine = [scale * x[sectors:sectors + 1, :] for x in current]
    for copy in coming:
        copy.wait()
    going = []
    for slot in range(slots):
        on_first, on_res, on_deep = [x[:, slot:slot + 1] for x in mine]
        state = on_first * start_ref[slot].astype(jnp.float32)
        state = state + on_res * res_ref[slot] + on_deep * deep_ref[slot]
        state = jnp.where(slot < live, state, 0.0).astype(jnp.bfloat16)
        state_ref[slot] = state
        spread[slot] = state.astype(jnp.float32)
        going.append(pltpu.make_async_copy(state_ref.at[slot], state_hbm.at[slot], sems.at[3, slot]))
        going[-1].start()
    for slot in range(slots):
        wide = jnp.concatenate(
            [spread[slot, pl.ds(s, BLK, stride=PHYS), :] for s in range(PHYS)], axis=1
        ).astype(jnp.bfloat16)
        product = lax.dot_general(
            wide, wide, (((1,), (1,)), ((), ())), preferred_element_type=jnp.float32
        )
        density_ref[slot] = product * (1.0 / ROWS)
        going.append(pltpu.make_async_copy(density_ref.at[slot], density_hbm.at[slot], sems.at[4, slot]))
        going[-1].start()
    for copy in going:
        copy.wait()


def from_behind(shard, axis, by):
    length = lax.axis_size(axis)
    return lax.ppermute(shard, axis, [(i, i + by) for i in range(length - by)])


def entering(decay, terms, axis):
    slots = decay.shape[0]
    own = jnp.concatenate([decay, terms], axis=0)
    other = lax.ppermute(own, axis, [(i, i ^ 1) for i in range(lax.axis_size(axis))])
    second = lax.axis_index(axis) % 2 == 1
    early, late = jnp.where(second, other, own), jnp.where(second, own, other)
    pair = jnp.concatenate(
        [early[:slots] * late[:slots], late[:slots] * early[slots:] + late[slots:]], axis=0
    )
    total = jnp.zeros_like(terms)
    for by in (6, 4, 2):
        earlier = from_behind(pair, axis, by)
        total = earlier[:slots] * total + earlier[slots:]
    return jnp.where(second, early[:slots] * total + early[slots:], total)


SMEM = pl.BlockSpec(memory_space=pltpu.SMEM)
VMEM = pl.BlockSpec(memory_space=pltpu.VMEM)
HBM = pl.BlockSpec(memory_space=pl.ANY)


def krylov_call(base, copies, live_count, region, before, offsets, operator, start, own, left, right, lanes):
    vectors = jax.ShapeDtypeStruct((GROUPED, ROWS, BLK), jnp.float32)
    head = base == 0
    kernel = functools.partial(krylov_kernel, base)
    operands = [live_count, region, offsets, start, own, left, right, lanes]
    operands += list(operator) if head else [operator, before]
    shapes = [jax.ShapeDtypeStruct((copies, BLK), jnp.float32), vectors, vectors]
    shapes += [jax.ShapeDtypeStruct((256, 256), jnp.bfloat16)] if head else []
    small = [pltpu.VMEM(x.shape, x.dtype) for x in (operator if head else [before])]
    return pl.pallas_call(
        kernel,
        in_specs=[SMEM, SMEM] + [HBM] * (len(operands) - 2),
        out_specs=[VMEM] + [HBM] * (len(shapes) - 1),
        out_shape=shapes,
        scratch_shapes=[
            pltpu.VMEM((GROUPED, ROWS, BLK), jnp.bfloat16),
            pltpu.VMEM((GROUPED, CHAN, BLK, BLK), jnp.bfloat16),
            pltpu.VMEM((GROUPED, CHAN, BLK, BLK), jnp.bfloat16),
            pltpu.VMEM((4 * BLK, 4 * BLK), jnp.bfloat16),
            pltpu.VMEM((GROUPED, ROWS, BLK), jnp.float32),
            pltpu.VMEM((GROUPED, ROWS, BLK), jnp.float32),
            pltpu.VMEM((GROUPED, BLK, CHAN * BLK), jnp.bfloat16),
            pltpu.VMEM((GROUPED, 16, 256, 256), jnp.bfloat16),
            pltpu.VMEM((GROUPED, CHAN * BLK, ROWS), jnp.bfloat16),
            pltpu.VMEM((GROUPED, ROWS, BLK), jnp.float32),
            pltpu.VMEM((GROUPED, ROWS, BLK), jnp.float32),
            pltpu.VMEM(offsets.shape, jnp.float32),
            pltpu.VMEM((256, 256), jnp.bfloat16),
            pltpu.SemaphoreType.DMA((12 + GROUPED,)),
        ] + small,
        compiler_params=pltpu.CompilerParams(vmem_limit_bytes=VMEM_LIMIT),
        cost_estimate=pl.CostEstimate(flops=10**10, bytes_accessed=1 << 22, transcendentals=0),
        name="krylov",
    )(*operands)


def rotate_call(sectors, live_count, every, sums, start, res, deep):
    slots = start.shape[0]
    return pl.pallas_call(
        functools.partial(rotate_kernel, math.sqrt(slots * sectors * ROWS * BLK), slots, sectors),
        in_specs=[SMEM] + [HBM] * (3 + 2 * (slots // GROUPED)),
        out_specs=[HBM, HBM, VMEM],
        out_shape=[
            jax.ShapeDtypeStruct((slots, ROWS, BLK), jnp.bfloat16),
            jax.ShapeDtypeStruct((slots, BLK, BLK), jnp.float32),
            jax.ShapeDtypeStruct((1, 1), jnp.float32),
        ],
        scratch_shapes=[
            pltpu.VMEM((sectors + 8, BLK), jnp.float32),
            pltpu.VMEM((slots, ROWS, BLK), jnp.bfloat16),
            pltpu.VMEM((slots, ROWS, BLK), jnp.float32),
            pltpu.VMEM((slots, ROWS, BLK), jnp.float32),
            pltpu.VMEM((slots, ROWS, BLK), jnp.bfloat16),
            pltpu.VMEM((slots, BLK, BLK), jnp.float32),
            pltpu.VMEM((slots, ROWS, BLK), jnp.float32),
            pltpu.SemaphoreType.DMA((5, slots)),
        ],
        compiler_params=pltpu.CompilerParams(vmem_limit_bytes=VMEM_LIMIT),
        name="rotate",
    )(live_count, every, sums, start, *res, *deep)


def body(start_state, left_env, right_env, mpo_tensor, decay, energy_terms, live_count):
    slots = start_state.shape[1]
    sectors = lax.axis_size("sector")
    start = start_state.reshape(slots, ROWS, BLK)
    arrived = [from_behind(left_env[0, at:at + GROUPED], "region", 1) for at in range(0, slots, GROUPED)]
    offsets = entering(decay[0], energy_terms[0], "region")
    region = lax.axis_index("region").reshape(1).astype(jnp.int32)
    mpo = mpo_tensor.reshape(CHAN * PHYS, PHYS * CHAN)
    lanes, rows, cols, same = constants()
    sums = None
    operator = (mpo, rows, cols, same)
    res, deep = [], []
    for base in range(0, slots, GROUPED):
        copies = sectors if base + GROUPED == slots else 1
        sums, res_one, deep_one, *made = krylov_call(
            base, copies, live_count, region, sums, offsets, operator,
            start, left_env[0], arrived[base // GROUPED], right_env[0], lanes,
        )
        operator = made[0] if made else operator
        res.append(res_one)
        deep.append(deep_one)
    every = lax.all_to_all(sums.reshape(sectors, 1, BLK), "sector", 0, 0).reshape(sectors, BLK)
    state, density, energy = rotate_call(sectors, live_count, every, sums, start, res, deep)
    return (state.reshape(start_state.shape), density[None], energy.reshape(1))


def solution(mesh):
    in_specs = (
        P("region", "sector", None, None, None),
        P("region", "sector", None, None, None),
        P("region", "sector", None, None, None),
        P(),
        P("region", "sector", None),
        P("region", "sector", None),
        P("region", "sector"),
    )
    out_specs = (
        P("region", "sector", None, None, None),
        P("region", "sector", None, None),
        P("region"),
    )
    return jax.shard_map(body, mesh=mesh, in_specs=in_specs, out_specs=out_specs, check_vma=False)
```

```python
import functools
import math

import jax
import jax.numpy as jnp
import numpy as np
from jax import lax
from jax.experimental import pallas as pl
from jax.experimental.pallas import tpu as pltpu
from jax.sharding import PartitionSpec as P

DAV = 2
EPS = 1e-06
BLK = 128
PHYS = 4
CHAN = 16
ROWS = BLK * PHYS
GROUP = 4
VMEM_LIMIT = 61 << 20
GROUPED = 2
STRIDE = 8

(NORM, SHIFT, RES, BACK, DIAG, DEEP, ON_F, ON_R, ON_D) = range(9)


def constants():
    lanes = np.zeros((4 * BLK, 4 * BLK), np.float32)
    for u in range(4):
        for a in range(BLK):
            lanes[u * BLK + a, (a // GROUP) * 16 + u * GROUP + a % GROUP] = 1.0
    rows = np.zeros((256, 64), np.float32)
    cols = np.zeros((64, 256), np.float32)
    same = np.zeros((256, 256), np.float32)
    for s in range(PHYS):
        for u in range(CHAN):
            for g in range(GROUP):
                rows[s * 64 + u * GROUP + g, u * PHYS + s] = 1.0
    for t in range(PHYS):
        for w in range(CHAN):
            for g in range(GROUP):
                cols[t * CHAN + w, w * 16 + g * PHYS + t] = 1.0
    index = np.arange(256)
    same[:, :] = (index[:, None] % GROUP) == ((index[None, :] // PHYS) % GROUP)
    return [jnp.asarray(m, jnp.bfloat16) for m in (lanes, rows, cols, same)]


def matmul(x, y):
    return jnp.dot(x, y, preferred_element_type=jnp.float32)


def total(x):
    return jnp.sum(jnp.sum(x, axis=0, keepdims=True), axis=1, keepdims=True)


def ratio(top, bottom):
    return jnp.where(bottom > 0.0, top / jnp.where(bottom > 0.0, bottom, 1.0), 0.0)


def krylov_kernel(
    base, live_ref, region_ref, offset_hbm, start_hbm, own_hbm, left_hbm, right_hbm, lanes_hbm, *refs
):
    head = base == 0
    if head:
        small_hbm, (sums_ref, res_hbm, deep_hbm, operator_hbm) = refs[:4], refs[4:8]
        refs = refs[8:]
    else:
        small_hbm, (sums_ref, res_hbm, deep_hbm) = refs[:2], refs[2:5]
        refs = refs[5:]
    (
        start_ref, left_ref, right_ref, lanes_ref, res_ref, deep_ref,
        left_lanes, first_half, second_half, spread, shift, offset_ref, operator_ref, sems, *small,
    ) = refs
    if not head:
        small = [operator_ref] + small
    group = range(start_ref.shape[0])

    def operate_right(i, vector):
        for pair in range(CHAN // 2):
            right = jnp.concatenate([right_ref[i, 2 * pair], right_ref[i, 2 * pair + 1]], axis=1)
            made = matmul(vector, right).astype(jnp.bfloat16)
            for j in range(2):
                w = 2 * pair + j
                for half in range(2):
                    part = made[half * 256:(half + 1) * 256, j * BLK:(j + 1) * BLK]
                    first_half[i, :, w * 16:(w + 1) * 16, half * BLK:(half + 1) * BLK] = part.reshape(16, 16, BLK)
        for g in range(16):
            made = matmul(operator_ref[...], first_half[i, g]).astype(jnp.bfloat16)
            for half in range(2):
                for s in range(PHYS):
                    for ug in range(4):
                        at = ug * 512 + (half * 16 + g) * 16
                        second_half[i, at:at + 16, s * BLK:(s + 1) * BLK] = made[
                            s * 64 + ug * 16:s * 64 + ug * 16 + 16, half * BLK:(half + 1) * BLK]

    def operate_left(i):
        made = matmul(left_lanes[i], second_half[i])
        for s in range(PHYS):
            spread[i, pl.ds(s, BLK, stride=PHYS), :] = made[:, s * BLK:(s + 1) * BLK]
        return spread[i]

    def order_lanes(i):
        for ug in range(4):
            four = jnp.concatenate([left_ref[i, 4 * ug + j] for j in range(4)], axis=1)
            left_lanes[i, :, ug * 512:(ug + 1) * 512] = matmul(four, lanes_ref[...]).astype(jnp.bfloat16)

    live = live_ref[0, 0]
    outer = region_ref[0] == 0
    lane = lax.broadcasted_iota(jnp.int32, (1, BLK), 1)

    @pl.when(base < live)
    def _():
        start_in = pltpu.make_async_copy(start_hbm.at[pl.ds(base, len(group))], start_ref, sems.at[0])
        right_in = [
            pltpu.make_async_copy(right_hbm.at[base + i], right_ref.at[i], sems.at[6 + i]) for i in group
        ]
        lanes_in = pltpu.make_async_copy(lanes_hbm, lanes_ref, sems.at[2])
        left_in = pltpu.make_async_copy(left_hbm, left_ref, sems.at[3])
        small_in = [
            pltpu.make_async_copy(hbm, ref, sems.at[6 + len(group) + k])
            for k, (hbm, ref) in enumerate(zip([offset_hbm] + list(small_hbm), [offset_ref] + small))
        ]
        for copy in small_in:
            copy.start()
        start_in.start()
        for copy in right_in:
            copy.start()
        lanes_in.start()

        @pl.when(outer)
        def _():
            pltpu.make_async_copy(own_hbm.at[pl.ds(base, len(group))], left_ref, sems.at[3]).start()

        @pl.when(jnp.logical_not(outer))
        def _():
            left_in.start()

        for copy in small_in:
            copy.wait()
        if head:
            mpo_ref, rows_ref, cols_ref, same_ref = small
            sums = jnp.zeros((1, BLK), jnp.float32)
            wide = matmul(rows_ref[...], mpo_ref[...]).astype(jnp.bfloat16)
            wide = matmul(wide, cols_ref[...]).astype(jnp.bfloat16)
            operator_ref[...] = wide * same_ref[...]
            operator_out = pltpu.make_async_copy(operator_ref, operator_hbm, sems.at[6 + len(group) + 5])
            operator_out.start()
        else:
            sums = small[1][...]

        def note(sums, i, quantity, value):
            slot = base + i
            return sums + jnp.where(jnp.logical_and(lane == quantity * STRIDE + slot, slot < live), value, 0.0)

        for i in group:
            column = jnp.broadcast_to(offset_ref[base + i:base + i + 1, :], (BLK, BLK)).T
            for s in range(PHYS):
                shift[i, pl.ds(s, BLK, stride=PHYS), :] = column
        res_out = pltpu.make_async_copy(res_ref, res_hbm, sems.at[4])
        deep_out = pltpu.make_async_copy(deep_ref, deep_hbm, sems.at[5])
        norm, res_norm = {}, {}

        start_in.wait()
        for i in group:
            right_in[i].wait()
            operate_right(i, start_ref[i])
        lanes_in.wait()
        left_in.wait()
        for i in group:
            order_lanes(i)
        for i in group:
            first = start_ref[i].astype(jnp.float32)
            image = operate_left(i) + shift[i] * first
            norm[i] = total(first * first)
            quotient = ratio(total(first * image), norm[i])
            res = image - quotient * first
            res_ref[i] = res
            res_norm[i] = total(res * res)
            sums = note(note(note(sums, i, NORM, norm[i]), i, SHIFT, quotient), i, RES, res_norm[i])

        res_out.start()
        for i in group:
            operate_right(i, res_ref[i].astype(jnp.bfloat16))
        for i in group:
            res = res_ref[i]
            first = start_ref[i].astype(jnp.float32)
            image = operate_left(i) + shift[i] * res.astype(jnp.bfloat16).astype(jnp.float32)
            back = ratio(total(first * image), norm[i])
            diag = ratio(total(res * image), res_norm[i])
            deep = image - back * first - diag * res
            deep_ref[i] = deep
            sums = note(note(note(sums, i, BACK, back), i, DIAG, diag), i, DEEP, total(deep * deep))

        deep_out.start()
        for i in group:
            operate_right(i, deep_ref[i].astype(jnp.bfloat16))
        for i in group:
            deep = deep_ref[i]
            image = operate_left(i) + shift[i] * deep.astype(jnp.bfloat16).astype(jnp.float32)
            sums = note(sums, i, ON_F, total(start_ref[i].astype(jnp.float32) * image))
            sums = note(sums, i, ON_R, total(res_ref[i] * image))
            sums = note(sums, i, ON_D, total(deep * image))
        sums_ref[...] = jnp.broadcast_to(sums, sums_ref.shape)
        res_out.wait()
        deep_out.wait()
        if head:
            operator_out.wait()

    if not head:

        @pl.when(base >= live)
        def _():
            before_in = pltpu.make_async_copy(small_hbm[1], small[1], sems.at[0])
            before_in.start()
            before_in.wait()
            sums_ref[...] = jnp.broadcast_to(small[1][...], sums_ref.shape)


def rotate_kernel(
    scale, slots, sectors, live_ref, all_hbm, own_hbm, start_hbm, *refs
):
    groups = slots // GROUPED
    res_hbm, deep_hbm = refs[:groups], refs[groups:2 * groups]
    state_hbm, density_hbm, energy_ref = refs[2 * groups:2 * groups + 3]
    table_ref, start_ref, res_ref, deep_ref, state_ref, density_ref, spread, sems = refs[2 * groups + 3:]
    live = live_ref[0, 0]
    tables = [
        pltpu.make_async_copy(all_hbm, table_ref.at[pl.ds(0, sectors)], sems.at[0, 0]),
        pltpu.make_async_copy(own_hbm.at[pl.ds(0, 8)], table_ref.at[pl.ds(sectors, 8)], sems.at[1, 0]),
    ]
    coming = [pltpu.make_async_copy(start_hbm, start_ref, sems.at[2, 0])]
    for group in range(groups):
        rows = pl.ds(group * GROUPED, GROUPED)
        coming.append(pltpu.make_async_copy(res_hbm[group], res_ref.at[rows], sems.at[0, 1 + group]))
        coming.append(pltpu.make_async_copy(deep_hbm[group], deep_ref.at[rows], sems.at[1, 1 + group]))
    for copy in tables + coming:
        copy.start()
    for copy in tables:
        copy.wait()
    table = table_ref[...]
    shape = (sectors + 8, BLK)
    row = lax.broadcasted_iota(jnp.int32, shape, 0)
    lane = lax.broadcasted_iota(jnp.int32, shape, 1)
    counted = jnp.logical_and(row < sectors, lane < STRIDE)

    def pick(quantity):
        return table if quantity == 0 else pltpu.roll(table, BLK - quantity * STRIDE, 1)

    def region_sum(x):
        return total(jnp.where(counted, x, 0.0))

    norm, shift, res_norm, back, diag, deep_norm, on_f, on_r, on_d = [pick(k) for k in range(9)]
    grams = (norm, res_norm, deep_norm)
    zero = jnp.zeros(shape, jnp.float32)

    def inner(x, y):
        made = x[0] * y[0] * grams[0]
        for k in (1, 2):
            made = made + x[k] * y[k] * grams[k]
        if len(y) > 3:
            made = made + y[3] * (x[0] * on_f + x[1] * on_r + x[2] * on_d)
        return region_sum(made)

    inverse = lax.rsqrt(region_sum(norm) + EPS)
    current = (zero + inverse, zero, zero)
    applied = (inverse * shift, zero + inverse, zero)
    for iteration in range(DAV):
        quotient = inner(current, applied)
        residual = tuple(x - quotient * y for x, y in zip(applied, current))
        resid_sq = inner(residual, residual)
        factor = lax.rsqrt(resid_sq + EPS)
        search = tuple(factor * x for x in residual)
        image = (search[0] * shift + search[1] * back, search[0] + search[1] * diag, search[1])
        if iteration == 1:
            image = image + (search[2],)
        curvature = inner(search, image)
        opposite = -2.0 * resid_sq * factor
        adjacent = curvature - quotient
        largest = jnp.maximum(jnp.abs(opposite), jnp.abs(adjacent))
        flat = largest == 0.0
        largest = jnp.where(flat, 1.0, largest)
        opposite = opposite / largest
        adjacent = jnp.where(flat, 1.0, adjacent / largest)
        length = jnp.sqrt(opposite * opposite + adjacent * adjacent)
        double_cos = jnp.abs(adjacent) / length
        double_sin = jnp.abs(opposite) / length
        large = jnp.sqrt(0.5 + 0.5 * double_cos)
        small = double_sin / (2.0 * large)
        ahead = adjacent >= 0.0
        cos_part = jnp.where(ahead, large, small)
        sin_part = -jnp.where(ahead, small, large)
        current = tuple(cos_part * x + sin_part * y for x, y in zip(current, search))
        turned = tuple(cos_part * x + sin_part * y for x, y in zip(applied, image))
        applied = turned + tuple(sin_part * y for y in image[3:])
    energy_ref[...] = jnp.broadcast_to(inner(current, applied), energy_ref.shape)
    mine = [scale * x[sectors:sectors + 1, :] for x in current]
    for copy in coming:
        copy.wait()
    going = []
    for slot in range(slots):
        on_first, on_res, on_deep = [x[:, slot:slot + 1] for x in mine]
        state = on_first * start_ref[slot].astype(jnp.float32)
        state = state + on_res * res_ref[slot] + on_deep * deep_ref[slot]
        state = jnp.where(slot < live, state, 0.0).astype(jnp.bfloat16)
        state_ref[slot] = state
        spread[slot] = state.astype(jnp.float32)
        going.append(pltpu.make_async_copy(state_ref.at[slot], state_hbm.at[slot], sems.at[3, slot]))
        going[-1].start()
    for slot in range(slots):
        wide = jnp.concatenate(
            [spread[slot, pl.ds(s, BLK, stride=PHYS), :] for s in range(PHYS)], axis=1
        ).astype(jnp.bfloat16)
        product = lax.dot_general(
            wide, wide, (((1,), (1,)), ((), ())), preferred_element_type=jnp.float32
        )
        density_ref[slot] = product * (1.0 / ROWS)
        going.append(pltpu.make_async_copy(density_ref.at[slot], density_hbm.at[slot], sems.at[4, slot]))
        going[-1].start()
    for copy in going:
        copy.wait()


def from_behind(shard, axis, by):
    length = lax.axis_size(axis)
    return lax.ppermute(shard, axis, [(i, i + by) for i in range(length - by)])


def entering(decay, terms, axis):
    slots = decay.shape[0]
    own = jnp.concatenate([decay, terms], axis=0)
    other = lax.ppermute(own, axis, [(i, i ^ 1) for i in range(lax.axis_size(axis))])
    second = lax.axis_index(axis) % 2 == 1
    early, late = jnp.where(second, other, own), jnp.where(second, own, other)
    pair = jnp.concatenate(
        [early[:slots] * late[:slots], late[:slots] * early[slots:] + late[slots:]], axis=0
    )
    total = jnp.zeros_like(terms)
    for by in (6, 4, 2):
        earlier = from_behind(pair, axis, by)
        total = earlier[:slots] * total + earlier[slots:]
    return jnp.where(second, early[:slots] * total + early[slots:], total)


SMEM = pl.BlockSpec(memory_space=pltpu.SMEM)
VMEM = pl.BlockSpec(memory_space=pltpu.VMEM)
HBM = pl.BlockSpec(memory_space=pl.ANY)


def krylov_call(base, copies, live_count, region, before, offsets, operator, start, own, left, right, lanes):
    vectors = jax.ShapeDtypeStruct((GROUPED, ROWS, BLK), jnp.float32)
    head = base == 0
    kernel = functools.partial(krylov_kernel, base)
    operands = [live_count, region, offsets, start, own, left, right, lanes]
    operands += list(operator) if head else [operator, before]
    shapes = [jax.ShapeDtypeStruct((copies, BLK), jnp.float32), vectors, vectors]
    shapes += [jax.ShapeDtypeStruct((256, 256), jnp.bfloat16)] if head else []
    small = [pltpu.VMEM(x.shape, x.dtype) for x in (operator if head else [before])]
    return pl.pallas_call(
        kernel,
        in_specs=[SMEM, SMEM] + [HBM] * (len(operands) - 2),
        out_specs=[VMEM] + [HBM] * (len(shapes) - 1),
        out_shape=shapes,
        scratch_shapes=[
            pltpu.VMEM((GROUPED, ROWS, BLK), jnp.bfloat16),
            pltpu.VMEM((GROUPED, CHAN, BLK, BLK), jnp.bfloat16),
            pltpu.VMEM((GROUPED, CHAN, BLK, BLK), jnp.bfloat16),
            pltpu.VMEM((4 * BLK, 4 * BLK), jnp.bfloat16),
            pltpu.VMEM((GROUPED, ROWS, BLK), jnp.float32),
            pltpu.VMEM((GROUPED, ROWS, BLK), jnp.float32),
            pltpu.VMEM((GROUPED, BLK, CHAN * BLK), jnp.bfloat16),
            pltpu.VMEM((GROUPED, 16, 256, 256), jnp.bfloat16),
            pltpu.VMEM((GROUPED, CHAN * BLK, ROWS), jnp.bfloat16),
            pltpu.VMEM((GROUPED, ROWS, BLK), jnp.float32),
            pltpu.VMEM((GROUPED, ROWS, BLK), jnp.float32),
            pltpu.VMEM(offsets.shape, jnp.float32),
            pltpu.VMEM((256, 256), jnp.bfloat16),
            pltpu.SemaphoreType.DMA((12 + GROUPED,)),
        ] + small,
        compiler_params=pltpu.CompilerParams(vmem_limit_bytes=VMEM_LIMIT),
        cost_estimate=pl.CostEstimate(flops=10**10, bytes_accessed=1 << 22, transcendentals=0),
        name="krylov",
    )(*operands)


def rotate_call(sectors, live_count, every, sums, start, res, deep):
    slots = start.shape[0]
    return pl.pallas_call(
        functools.partial(rotate_kernel, math.sqrt(slots * sectors * ROWS * BLK), slots, sectors),
        in_specs=[SMEM] + [HBM] * (3 + 2 * (slots // GROUPED)),
        out_specs=[HBM, HBM, VMEM],
        out_shape=[
            jax.ShapeDtypeStruct((slots, ROWS, BLK), jnp.bfloat16),
            jax.ShapeDtypeStruct((slots, BLK, BLK), jnp.float32),
            jax.ShapeDtypeStruct((1, 1), jnp.float32),
        ],
        scratch_shapes=[
            pltpu.VMEM((sectors + 8, BLK), jnp.float32),
            pltpu.VMEM((slots, ROWS, BLK), jnp.bfloat16),
            pltpu.VMEM((slots, ROWS, BLK), jnp.float32),
            pltpu.VMEM((slots, ROWS, BLK), jnp.float32),
            pltpu.VMEM((slots, ROWS, BLK), jnp.bfloat16),
            pltpu.VMEM((slots, BLK, BLK), jnp.float32),
            pltpu.VMEM((slots, ROWS, BLK), jnp.float32),
            pltpu.SemaphoreType.DMA((5, slots)),
        ],
        compiler_params=pltpu.CompilerParams(vmem_limit_bytes=VMEM_LIMIT),
        name="rotate",
    )(live_count, every, sums, start, *res, *deep)


def body(start_state, left_env, right_env, mpo_tensor, decay, energy_terms, live_count):
    slots = start_state.shape[1]
    sectors = lax.axis_size("sector")
    start = start_state.reshape(slots, ROWS, BLK)
    arrived = [from_behind(left_env[0, at:at + GROUPED], "region", 1) for at in range(0, slots, GROUPED)]
    offsets = entering(decay[0], energy_terms[0], "region")
    region = lax.axis_index("region").reshape(1).astype(jnp.int32)
    mpo = mpo_tensor.reshape(CHAN * PHYS, PHYS * CHAN)
    lanes, rows, cols, same = constants()
    sums = None
    operator = (mpo, rows, cols, same)
    res, deep = [], []
    for base in range(0, slots, GROUPED):
        copies = sectors if base + GROUPED == slots else 1
        sums, res_one, deep_one, *made = krylov_call(
            base, copies, live_count, region, sums, offsets, operator,
            start, left_env[0], arrived[base // GROUPED], right_env[0], lanes,
        )
        operator = made[0] if made else operator
        res.append(res_one)
        deep.append(deep_one)
    every = lax.all_to_all(sums.reshape(sectors, 1, BLK), "sector", 0, 0).reshape(sectors, BLK)
    state, density, energy = rotate_call(sectors, live_count, every, sums, start, res, deep)
    return (state.reshape(start_state.shape), density[None], energy.reshape(1))


def solution(mesh):
    in_specs = (
        P("region", "sector", None, None, None),
        P("region", "sector", None, None, None),
        P("region", "sector", None, None, None),
        P(),
        P("region", "sector", None),
        P("region", "sector", None),
        P("region", "sector"),
    )
    out_specs = (
        P("region", "sector", None, None, None),
        P("region", "sector", None, None),
        P("region"),
    )
    return jax.shard_map(body, mesh=mesh, in_specs=in_specs, out_specs=out_specs, check_vma=False)
```

```python
import functools
import math

import jax
import jax.numpy as jnp
import numpy as np
from jax import lax
from jax.experimental import pallas as pl
from jax.experimental.pallas import tpu as pltpu
from jax.sharding import PartitionSpec as P

DAV = 2
EPS = 1e-06
BLK = 128
PHYS = 4
CHAN = 16
ROWS = BLK * PHYS
GROUP = 4
VMEM_LIMIT = 50 << 20
GROUPED = 2
STRIDE = 8

(NORM, SHIFT, RES, BACK, DIAG, DEEP, ON_F, ON_R, ON_D) = range(9)


def constants():
    lanes = np.zeros((4 * BLK, 4 * BLK), np.float32)
    for u in range(4):
        for a in range(BLK):
            lanes[u * BLK + a, (a // GROUP) * 16 + u * GROUP + a % GROUP] = 1.0
    rows = np.zeros((256, 64), np.float32)
    cols = np.zeros((64, 256), np.float32)
    same = np.zeros((256, 256), np.float32)
    for s in range(PHYS):
        for u in range(CHAN):
            for g in range(GROUP):
                rows[s * 64 + u * GROUP + g, u * PHYS + s] = 1.0
    for t in range(PHYS):
        for w in range(CHAN):
            for g in range(GROUP):
                cols[t * CHAN + w, w * 16 + g * PHYS + t] = 1.0
    index = np.arange(256)
    same[:, :] = (index[:, None] % GROUP) == ((index[None, :] // PHYS) % GROUP)
    return [jnp.asarray(m, jnp.bfloat16) for m in (lanes, rows, cols, same)]


def matmul(x, y):
    return jnp.dot(x, y, preferred_element_type=jnp.float32)


def total(x):
    return jnp.sum(jnp.sum(x, axis=0, keepdims=True), axis=1, keepdims=True)


def ratio(top, bottom):
    return jnp.where(bottom > 0.0, top / jnp.where(bottom > 0.0, bottom, 1.0), 0.0)


def krylov_kernel(
    base, live_ref, region_ref, offset_hbm, start_hbm, own_hbm, left_hbm, right_hbm, lanes_hbm, *refs
):
    head = base == 0
    if head:
        small_hbm, (sums_ref, res_hbm, deep_hbm, operator_hbm) = refs[:4], refs[4:8]
        refs = refs[8:]
    else:
        small_hbm, (sums_ref, res_hbm, deep_hbm) = refs[:2], refs[2:5]
        refs = refs[5:]
    (
        start_ref, left_ref, right_ref, lanes_ref, res_ref, deep_ref,
        left_lanes, first_half, second_half, spread, shift, offset_ref, operator_ref, sems, *small,
    ) = refs
    if not head:
        small = [operator_ref] + small
    group = range(start_ref.shape[0])

    def operate_right(i, vector):
        for pair in range(CHAN // 2):
            right = jnp.concatenate([right_ref[i, 2 * pair], right_ref[i, 2 * pair + 1]], axis=1)
            made = matmul(vector, right).astype(jnp.bfloat16)
            for j in range(2):
                w = 2 * pair + j
                for half in range(2):
                    part = made[half * 256:(half + 1) * 256, j * BLK:(j + 1) * BLK]
                    first_half[i, :, w * 16:(w + 1) * 16, half * BLK:(half + 1) * BLK] = part.reshape(16, 16, BLK)
        for g in range(16):
            made = matmul(operator_ref[...], first_half[i, g]).astype(jnp.bfloat16)
            for half in range(2):
                for s in range(PHYS):
                    for ug in range(4):
                        at = ug * 512 + (half * 16 + g) * 16
                        second_half[i, at:at + 16, s * BLK:(s + 1) * BLK] = made[
                            s * 64 + ug * 16:s * 64 + ug * 16 + 16, half * BLK:(half + 1) * BLK]

    def operate_left(i):
        made = matmul(left_lanes[i], second_half[i])
        for s in range(PHYS):
            spread[i, pl.ds(s, BLK, stride=PHYS), :] = made[:, s * BLK:(s + 1) * BLK]
        return spread[i]

    def order_lanes(i):
        for ug in range(4):
            four = jnp.concatenate([left_ref[i, 4 * ug + j] for j in range(4)], axis=1)
            left_lanes[i, :, ug * 512:(ug + 1) * 512] = matmul(four, lanes_ref[...]).astype(jnp.bfloat16)

    live = live_ref[0, 0]
    outer = region_ref[0] == 0
    lane = lax.broadcasted_iota(jnp.int32, (1, BLK), 1)

    @pl.when(base < live)
    def _():
        start_in = pltpu.make_async_copy(start_hbm.at[pl.ds(base, len(group))], start_ref, sems.at[0])
        right_in = [
            pltpu.make_async_copy(right_hbm.at[base + i], right_ref.at[i], sems.at[6 + i]) for i in group
        ]
        lanes_in = pltpu.make_async_copy(lanes_hbm, lanes_ref, sems.at[2])
        left_in = pltpu.make_async_copy(left_hbm, left_ref, sems.at[3])
        small_in = [
            pltpu.make_async_copy(hbm, ref, sems.at[6 + len(group) + k])
            for k, (hbm, ref) in enumerate(zip([offset_hbm] + list(small_hbm), [offset_ref] + small))
        ]
        for copy in small_in:
            copy.start()
        start_in.start()
        for copy in right_in:
            copy.start()
        lanes_in.start()

        @pl.when(outer)
        def _():
            pltpu.make_async_copy(own_hbm.at[pl.ds(base, len(group))], left_ref, sems.at[3]).start()

        @pl.when(jnp.logical_not(outer))
        def _():
            left_in.start()

        for copy in small_in:
            copy.wait()
        if head:
            mpo_ref, rows_ref, cols_ref, same_ref = small
            sums = jnp.zeros((1, BLK), jnp.float32)
            wide = matmul(rows_ref[...], mpo_ref[...]).astype(jnp.bfloat16)
            wide = matmul(wide, cols_ref[...]).astype(jnp.bfloat16)
            operator_ref[...] = wide * same_ref[...]
            operator_out = pltpu.make_async_copy(operator_ref, operator_hbm, sems.at[6 + len(group) + 5])
            operator_out.start()
        else:
            sums = small[1][...]

        def note(sums, i, quantity, value):
            slot = base + i
            return sums + jnp.where(jnp.logical_and(lane == quantity * STRIDE + slot, slot < live), value, 0.0)

        for i in group:
            column = jnp.broadcast_to(offset_ref[base + i:base + i + 1, :], (BLK, BLK)).T
            for s in range(PHYS):
                shift[i, pl.ds(s, BLK, stride=PHYS), :] = column
        res_out = pltpu.make_async_copy(res_ref, res_hbm, sems.at[4])
        deep_out = pltpu.make_async_copy(deep_ref, deep_hbm, sems.at[5])
        norm, res_norm = {}, {}

        start_in.wait()
        for i in group:
            right_in[i].wait()
            operate_right(i, start_ref[i])
        lanes_in.wait()
        left_in.wait()
        for i in group:
            order_lanes(i)
        for i in group:
            first = start_ref[i].astype(jnp.float32)
            image = operate_left(i) + shift[i] * first
            norm[i] = total(first * first)
            quotient = ratio(total(first * image), norm[i])
            res = image - quotient * first
            res_ref[i] = res
            res_norm[i] = total(res * res)
            sums = note(note(note(sums, i, NORM, norm[i]), i, SHIFT, quotient), i, RES, res_norm[i])

        res_out.start()
        for i in group:
            operate_right(i, res_ref[i].astype(jnp.bfloat16))
        for i in group:
            res = res_ref[i]
            first = start_ref[i].astype(jnp.float32)
            image = operate_left(i) + shift[i] * res.astype(jnp.bfloat16).astype(jnp.float32)
            back = ratio(total(first * image), norm[i])
            diag = ratio(total(res * image), res_norm[i])
            deep = image - back * first - diag * res
            deep_ref[i] = deep
            sums = note(note(note(sums, i, BACK, back), i, DIAG, diag), i, DEEP, total(deep * deep))

        deep_out.start()
        for i in group:
            operate_right(i, deep_ref[i].astype(jnp.bfloat16))
        for i in group:
            deep = deep_ref[i]
            image = operate_left(i) + shift[i] * deep.astype(jnp.bfloat16).astype(jnp.float32)
            sums = note(sums, i, ON_F, total(start_ref[i].astype(jnp.float32) * image))
            sums = note(sums, i, ON_R, total(res_ref[i] * image))
            sums = note(sums, i, ON_D, total(deep * image))
        sums_ref[...] = jnp.broadcast_to(sums, sums_ref.shape)
        res_out.wait()
        deep_out.wait()
        if head:
            operator_out.wait()

    if not head:

        @pl.when(base >= live)
        def _():
            before_in = pltpu.make_async_copy(small_hbm[1], small[1], sems.at[0])
            before_in.start()
            before_in.wait()
            sums_ref[...] = jnp.broadcast_to(small[1][...], sums_ref.shape)


def rotate_kernel(
    scale, slots, sectors, live_ref, all_hbm, own_hbm, start_hbm, *refs
):
    groups = slots // GROUPED
    res_hbm, deep_hbm = refs[:groups], refs[groups:2 * groups]
    state_hbm, density_hbm, energy_ref = refs[2 * groups:2 * groups + 3]
    table_ref, start_ref, res_ref, deep_ref, state_ref, density_ref, spread, sems = refs[2 * groups + 3:]
    live = live_ref[0, 0]
    tables = [
        pltpu.make_async_copy(all_hbm, table_ref.at[pl.ds(0, sectors)], sems.at[0, 0]),
        pltpu.make_async_copy(own_hbm.at[pl.ds(0, 8)], table_ref.at[pl.ds(sectors, 8)], sems.at[1, 0]),
    ]
    coming = [pltpu.make_async_copy(start_hbm, start_ref, sems.at[2, 0])]
    for group in range(groups):
        rows = pl.ds(group * GROUPED, GROUPED)
        coming.append(pltpu.make_async_copy(res_hbm[group], res_ref.at[rows], sems.at[0, 1 + group]))
        coming.append(pltpu.make_async_copy(deep_hbm[group], deep_ref.at[rows], sems.at[1, 1 + group]))
    for copy in tables + coming:
        copy.start()
    for copy in tables:
        copy.wait()
    table = table_ref[...]
    shape = (sectors + 8, BLK)
    row = lax.broadcasted_iota(jnp.int32, shape, 0)
    lane = lax.broadcasted_iota(jnp.int32, shape, 1)
    counted = jnp.logical_and(row < sectors, lane < STRIDE)

    def pick(quantity):
        return table if quantity == 0 else pltpu.roll(table, BLK - quantity * STRIDE, 1)

    def region_sum(x):
        return total(jnp.where(counted, x, 0.0))

    norm, shift, res_norm, back, diag, deep_norm, on_f, on_r, on_d = [pick(k) for k in range(9)]
    grams = (norm, res_norm, deep_norm)
    zero = jnp.zeros(shape, jnp.float32)

    def inner(x, y):
        made = x[0] * y[0] * grams[0]
        for k in (1, 2):
            made = made + x[k] * y[k] * grams[k]
        if len(y) > 3:
            made = made + y[3] * (x[0] * on_f + x[1] * on_r + x[2] * on_d)
        return region_sum(made)

    inverse = lax.rsqrt(region_sum(norm) + EPS)
    current = (zero + inverse, zero, zero)
    applied = (inverse * shift, zero + inverse, zero)
    for iteration in range(DAV):
        quotient = inner(current, applied)
        residual = tuple(x - quotient * y for x, y in zip(applied, current))
        resid_sq = inner(residual, residual)
        factor = lax.rsqrt(resid_sq + EPS)
        search = tuple(factor * x for x in residual)
        image = (search[0] * shift + search[1] * back, search[0] + search[1] * diag, search[1])
        if iteration == 1:
            image = image + (search[2],)
        curvature = inner(search, image)
        opposite = -2.0 * resid_sq * factor
        adjacent = curvature - quotient
        largest = jnp.maximum(jnp.abs(opposite), jnp.abs(adjacent))
        flat = largest == 0.0
        largest = jnp.where(flat, 1.0, largest)
        opposite = opposite / largest
        adjacent = jnp.where(flat, 1.0, adjacent / largest)
        length = jnp.sqrt(opposite * opposite + adjacent * adjacent)
        double_cos = jnp.abs(adjacent) / length
        double_sin = jnp.abs(opposite) / length
        large = jnp.sqrt(0.5 + 0.5 * double_cos)
        small = double_sin / (2.0 * large)
        ahead = adjacent >= 0.0
        cos_part = jnp.where(ahead, large, small)
        sin_part = -jnp.where(ahead, small, large)
        current = tuple(cos_part * x + sin_part * y for x, y in zip(current, search))
        turned = tuple(cos_part * x + sin_part * y for x, y in zip(applied, image))
        applied = turned + tuple(sin_part * y for y in image[3:])
    energy_ref[...] = jnp.broadcast_to(inner(current, applied), energy_ref.shape)
    mine = [scale * x[sectors:sectors + 1, :] for x in current]
    for copy in coming:
        copy.wait()
    going = []
    for slot in range(slots):
        on_first, on_res, on_deep = [x[:, slot:slot + 1] for x in mine]
        state = on_first * start_ref[slot].astype(jnp.float32)
        state = state + on_res * res_ref[slot] + on_deep * deep_ref[slot]
        state = jnp.where(slot < live, state, 0.0).astype(jnp.bfloat16)
        state_ref[slot] = state
        spread[slot] = state.astype(jnp.float32)
        going.append(pltpu.make_async_copy(state_ref.at[slot], state_hbm.at[slot], sems.at[3, slot]))
        going[-1].start()
    for slot in range(slots):
        wide = jnp.concatenate(
            [spread[slot, pl.ds(s, BLK, stride=PHYS), :] for s in range(PHYS)], axis=1
        ).astype(jnp.bfloat16)
        product = lax.dot_general(
            wide, wide, (((1,), (1,)), ((), ())), preferred_element_type=jnp.float32
        )
        density_ref[slot] = product * (1.0 / ROWS)
        going.append(pltpu.make_async_copy(density_ref.at[slot], density_hbm.at[slot], sems.at[4, slot]))
        going[-1].start()
    for copy in going:
        copy.wait()


def from_behind(shard, axis, by):
    length = lax.axis_size(axis)
    return lax.ppermute(shard, axis, [(i, i + by) for i in range(length - by)])


def entering(decay, terms, axis):
    slots = decay.shape[0]
    own = jnp.concatenate([decay, terms], axis=0)
    other = lax.ppermute(own, axis, [(i, i ^ 1) for i in range(lax.axis_size(axis))])
    second = lax.axis_index(axis) % 2 == 1
    early, late = jnp.where(second, other, own), jnp.where(second, own, other)
    pair = jnp.concatenate(
        [early[:slots] * late[:slots], late[:slots] * early[slots:] + late[slots:]], axis=0
    )
    total = jnp.zeros_like(terms)
    for by in (6, 4, 2):
        earlier = from_behind(pair, axis, by)
        total = earlier[:slots] * total + earlier[slots:]
    return jnp.where(second, early[:slots] * total + early[slots:], total)


SMEM = pl.BlockSpec(memory_space=pltpu.SMEM)
VMEM = pl.BlockSpec(memory_space=pltpu.VMEM)
HBM = pl.BlockSpec(memory_space=pl.ANY)


def krylov_call(base, copies, live_count, region, before, offsets, operator, start, own, left, right, lanes):
    vectors = jax.ShapeDtypeStruct((GROUPED, ROWS, BLK), jnp.float32)
    head = base == 0
    kernel = functools.partial(krylov_kernel, base)
    operands = [live_count, region, offsets, start, own, left, right, lanes]
    operands += list(operator) if head else [operator, before]
    shapes = [jax.ShapeDtypeStruct((copies, BLK), jnp.float32), vectors, vectors]
    shapes += [jax.ShapeDtypeStruct((256, 256), jnp.bfloat16)] if head else []
    small = [pltpu.VMEM(x.shape, x.dtype) for x in (operator if head else [before])]
    return pl.pallas_call(
        kernel,
        in_specs=[SMEM, SMEM] + [HBM] * (len(operands) - 2),
        out_specs=[VMEM] + [HBM] * (len(shapes) - 1),
        out_shape=shapes,
        scratch_shapes=[
            pltpu.VMEM((GROUPED, ROWS, BLK), jnp.bfloat16),
            pltpu.VMEM((GROUPED, CHAN, BLK, BLK), jnp.bfloat16),
            pltpu.VMEM((GROUPED, CHAN, BLK, BLK), jnp.bfloat16),
            pltpu.VMEM((4 * BLK, 4 * BLK), jnp.bfloat16),
            pltpu.VMEM((GROUPED, ROWS, BLK), jnp.float32),
            pltpu.VMEM((GROUPED, ROWS, BLK), jnp.float32),
            pltpu.VMEM((GROUPED, BLK, CHAN * BLK), jnp.bfloat16),
            pltpu.VMEM((GROUPED, 16, 256, 256), jnp.bfloat16),
            pltpu.VMEM((GROUPED, CHAN * BLK, ROWS), jnp.bfloat16),
            pltpu.VMEM((GROUPED, ROWS, BLK), jnp.float32),
            pltpu.VMEM((GROUPED, ROWS, BLK), jnp.float32),
            pltpu.VMEM(offsets.shape, jnp.float32),
            pltpu.VMEM((256, 256), jnp.bfloat16),
            pltpu.SemaphoreType.DMA((12 + GROUPED,)),
        ] + small,
        compiler_params=pltpu.CompilerParams(vmem_limit_bytes=VMEM_LIMIT),
        cost_estimate=pl.CostEstimate(flops=10**10, bytes_accessed=1 << 22, transcendentals=0),
        name="krylov",
    )(*operands)


def rotate_call(sectors, live_count, every, sums, start, res, deep):
    slots = start.shape[0]
    return pl.pallas_call(
        functools.partial(rotate_kernel, math.sqrt(slots * sectors * ROWS * BLK), slots, sectors),
        in_specs=[SMEM] + [HBM] * (3 + 2 * (slots // GROUPED)),
        out_specs=[HBM, HBM, VMEM],
        out_shape=[
            jax.ShapeDtypeStruct((slots, ROWS, BLK), jnp.bfloat16),
            jax.ShapeDtypeStruct((slots, BLK, BLK), jnp.float32),
            jax.ShapeDtypeStruct((1, 1), jnp.float32),
        ],
        scratch_shapes=[
            pltpu.VMEM((sectors + 8, BLK), jnp.float32),
            pltpu.VMEM((slots, ROWS, BLK), jnp.bfloat16),
            pltpu.VMEM((slots, ROWS, BLK), jnp.float32),
            pltpu.VMEM((slots, ROWS, BLK), jnp.float32),
            pltpu.VMEM((slots, ROWS, BLK), jnp.bfloat16),
            pltpu.VMEM((slots, BLK, BLK), jnp.float32),
            pltpu.VMEM((slots, ROWS, BLK), jnp.float32),
            pltpu.SemaphoreType.DMA((5, slots)),
        ],
        compiler_params=pltpu.CompilerParams(vmem_limit_bytes=VMEM_LIMIT),
        name="rotate",
    )(live_count, every, sums, start, *res, *deep)


def body(start_state, left_env, right_env, mpo_tensor, decay, energy_terms, live_count):
    slots = start_state.shape[1]
    sectors = lax.axis_size("sector")
    start = start_state.reshape(slots, ROWS, BLK)
    arrived = [from_behind(left_env[0, at:at + GROUPED], "region", 1) for at in range(0, slots, GROUPED)]
    offsets = entering(decay[0], energy_terms[0], "region")
    region = lax.axis_index("region").reshape(1).astype(jnp.int32)
    mpo = mpo_tensor.reshape(CHAN * PHYS, PHYS * CHAN)
    lanes, rows, cols, same = constants()
    sums = None
    operator = (mpo, rows, cols, same)
    res, deep = [], []
    for base in range(0, slots, GROUPED):
        copies = sectors if base + GROUPED == slots else 1
        sums, res_one, deep_one, *made = krylov_call(
            base, copies, live_count, region, sums, offsets, operator,
            start, left_env[0], arrived[base // GROUPED], right_env[0], lanes,
        )
        operator = made[0] if made else operator
        res.append(res_one)
        deep.append(deep_one)
    every = lax.all_to_all(sums.reshape(sectors, 1, BLK), "sector", 0, 0).reshape(sectors, BLK)
    state, density, energy = rotate_call(sectors, live_count, every, sums, start, res, deep)
    return (state.reshape(start_state.shape), density[None], energy.reshape(1))


def solution(mesh):
    in_specs = (
        P("region", "sector", None, None, None),
        P("region", "sector", None, None, None),
        P("region", "sector", None, None, None),
        P(),
        P("region", "sector", None),
        P("region", "sector", None),
        P("region", "sector"),
    )
    out_specs = (
        P("region", "sector", None, None, None),
        P("region", "sector", None, None),
        P("region"),
    )
    return jax.shard_map(body, mesh=mesh, in_specs=in_specs, out_specs=out_specs, check_vma=False)
```

```python
import functools
import math

import jax
import jax.numpy as jnp
import numpy as np
from jax import lax
from jax.experimental import pallas as pl
from jax.experimental.pallas import tpu as pltpu
from jax.sharding import PartitionSpec as P

DAV = 2
EPS = 1e-06
BLK = 128
PHYS = 4
CHAN = 16
ROWS = BLK * PHYS
GROUP = 4
VMEM_LIMIT = 52 << 20
GROUPED = 2
STRIDE = 8

(NORM, SHIFT, RES, BACK, DIAG, DEEP, ON_F, ON_R, ON_D) = range(9)


def constants():
    lanes = np.zeros((4 * BLK, 4 * BLK), np.float32)
    for u in range(4):
        for a in range(BLK):
            lanes[u * BLK + a, (a // GROUP) * 16 + u * GROUP + a % GROUP] = 1.0
    rows = np.zeros((256, 64), np.float32)
    cols = np.zeros((64, 256), np.float32)
    same = np.zeros((256, 256), np.float32)
    for s in range(PHYS):
        for u in range(CHAN):
            for g in range(GROUP):
                rows[s * 64 + u * GROUP + g, u * PHYS + s] = 1.0
    for t in range(PHYS):
        for w in range(CHAN):
            for g in range(GROUP):
                cols[t * CHAN + w, w * 16 + g * PHYS + t] = 1.0
    index = np.arange(256)
    same[:, :] = (index[:, None] % GROUP) == ((index[None, :] // PHYS) % GROUP)
    return [jnp.asarray(m, jnp.bfloat16) for m in (lanes, rows, cols, same)]


def matmul(x, y):
    return jnp.dot(x, y, preferred_element_type=jnp.float32)


def total(x):
    return jnp.sum(jnp.sum(x, axis=0, keepdims=True), axis=1, keepdims=True)


def ratio(top, bottom):
    return jnp.where(bottom > 0.0, top / jnp.where(bottom > 0.0, bottom, 1.0), 0.0)


def krylov_kernel(
    base, live_ref, region_ref, offset_hbm, start_hbm, own_hbm, left_hbm, right_hbm, lanes_hbm, *refs
):
    head = base == 0
    if head:
        small_hbm, (sums_ref, res_hbm, deep_hbm, operator_hbm) = refs[:4], refs[4:8]
        refs = refs[8:]
    else:
        small_hbm, (sums_ref, res_hbm, deep_hbm) = refs[:2], refs[2:5]
        refs = refs[5:]
    (
        start_ref, left_ref, right_ref, lanes_ref, res_ref, deep_ref,
        left_lanes, first_half, second_half, spread, shift, offset_ref, operator_ref, sems, *small,
    ) = refs
    if not head:
        small = [operator_ref] + small
    group = range(start_ref.shape[0])

    def operate_right(i, vector):
        for pair in range(CHAN // 2):
            right = jnp.concatenate([right_ref[i, 2 * pair], right_ref[i, 2 * pair + 1]], axis=1)
            made = matmul(vector, right).astype(jnp.bfloat16)
            for j in range(2):
                w = 2 * pair + j
                for half in range(2):
                    part = made[half * 256:(half + 1) * 256, j * BLK:(j + 1) * BLK]
                    first_half[i, :, w * 16:(w + 1) * 16, half * BLK:(half + 1) * BLK] = part.reshape(16, 16, BLK)
        for g in range(16):
            made = matmul(operator_ref[...], first_half[i, g]).astype(jnp.bfloat16)
            for half in range(2):
                for s in range(PHYS):
                    for ug in range(4):
                        at = ug * 512 + (half * 16 + g) * 16
                        second_half[i, at:at + 16, s * BLK:(s + 1) * BLK] = made[
                            s * 64 + ug * 16:s * 64 + ug * 16 + 16, half * BLK:(half + 1) * BLK]

    def operate_left(i):
        made = matmul(left_lanes[i], second_half[i])
        for s in range(PHYS):
            spread[i, pl.ds(s, BLK, stride=PHYS), :] = made[:, s * BLK:(s + 1) * BLK]
        return spread[i]

    def order_lanes(i):
        for ug in range(4):
            four = jnp.concatenate([left_ref[i, 4 * ug + j] for j in range(4)], axis=1)
            left_lanes[i, :, ug * 512:(ug + 1) * 512] = matmul(four, lanes_ref[...]).astype(jnp.bfloat16)

    live = live_ref[0, 0]
    outer = region_ref[0] == 0
    lane = lax.broadcasted_iota(jnp.int32, (1, BLK), 1)

    @pl.when(base < live)
    def _():
        start_in = pltpu.make_async_copy(start_hbm.at[pl.ds(base, len(group))], start_ref, sems.at[0])
        right_in = [
            pltpu.make_async_copy(right_hbm.at[base + i], right_ref.at[i], sems.at[6 + i]) for i in group
        ]
        lanes_in = pltpu.make_async_copy(lanes_hbm, lanes_ref, sems.at[2])
        left_in = pltpu.make_async_copy(left_hbm, left_ref, sems.at[3])
        small_in = [
            pltpu.make_async_copy(hbm, ref, sems.at[6 + len(group) + k])
            for k, (hbm, ref) in enumerate(zip([offset_hbm] + list(small_hbm), [offset_ref] + small))
        ]
        for copy in small_in:
            copy.start()
        start_in.start()
        for copy in right_in:
            copy.start()
        lanes_in.start()

        @pl.when(outer)
        def _():
            pltpu.make_async_copy(own_hbm.at[pl.ds(base, len(group))], left_ref, sems.at[3]).start()

        @pl.when(jnp.logical_not(outer))
        def _():
            left_in.start()

        for copy in small_in:
            copy.wait()
        if head:
            mpo_ref, rows_ref, cols_ref, same_ref = small
            sums = jnp.zeros((1, BLK), jnp.float32)
            wide = matmul(rows_ref[...], mpo_ref[...]).astype(jnp.bfloat16)
            wide = matmul(wide, cols_ref[...]).astype(jnp.bfloat16)
            operator_ref[...] = wide * same_ref[...]
            operator_out = pltpu.make_async_copy(operator_ref, operator_hbm, sems.at[6 + len(group) + 5])
            operator_out.start()
        else:
            sums = small[1][...]

        def note(sums, i, quantity, value):
            slot = base + i
            return sums + jnp.where(jnp.logical_and(lane == quantity * STRIDE + slot, slot < live), value, 0.0)

        for i in group:
            column = jnp.broadcast_to(offset_ref[base + i:base + i + 1, :], (BLK, BLK)).T
            for s in range(PHYS):
                shift[i, pl.ds(s, BLK, stride=PHYS), :] = column
        res_out = pltpu.make_async_copy(res_ref, res_hbm, sems.at[4])
        deep_out = pltpu.make_async_copy(deep_ref, deep_hbm, sems.at[5])
        norm, res_norm = {}, {}

        start_in.wait()
        for i in group:
            right_in[i].wait()
            operate_right(i, start_ref[i])
        lanes_in.wait()
        left_in.wait()
        for i in group:
            order_lanes(i)
        for i in group:
            first = start_ref[i].astype(jnp.float32)
            image = operate_left(i) + shift[i] * first
            norm[i] = total(first * first)
            quotient = ratio(total(first * image), norm[i])
            res = image - quotient * first
            res_ref[i] = res
            res_norm[i] = total(res * res)
            sums = note(note(note(sums, i, NORM, norm[i]), i, SHIFT, quotient), i, RES, res_norm[i])

        res_out.start()
        for i in group:
            operate_right(i, res_ref[i].astype(jnp.bfloat16))
        for i in group:
            res = res_ref[i]
            first = start_ref[i].astype(jnp.float32)
            image = operate_left(i) + shift[i] * res.astype(jnp.bfloat16).astype(jnp.float32)
            back = ratio(total(first * image), norm[i])
            diag = ratio(total(res * image), res_norm[i])
            deep = image - back * first - diag * res
            deep_ref[i] = deep
            sums = note(note(note(sums, i, BACK, back), i, DIAG, diag), i, DEEP, total(deep * deep))

        deep_out.start()
        for i in group:
            operate_right(i, deep_ref[i].astype(jnp.bfloat16))
        for i in group:
            deep = deep_ref[i]
            image = operate_left(i) + shift[i] * deep.astype(jnp.bfloat16).astype(jnp.float32)
            sums = note(sums, i, ON_F, total(start_ref[i].astype(jnp.float32) * image))
            sums = note(sums, i, ON_R, total(res_ref[i] * image))
            sums = note(sums, i, ON_D, total(deep * image))
        sums_ref[...] = jnp.broadcast_to(sums, sums_ref.shape)
        res_out.wait()
        deep_out.wait()
        if head:
            operator_out.wait()

    if not head:

        @pl.when(base >= live)
        def _():
            before_in = pltpu.make_async_copy(small_hbm[1], small[1], sems.at[0])
            before_in.start()
            before_in.wait()
            sums_ref[...] = jnp.broadcast_to(small[1][...], sums_ref.shape)


def rotate_kernel(
    scale, slots, sectors, live_ref, all_hbm, own_hbm, start_hbm, *refs
):
    groups = slots // GROUPED
    res_hbm, deep_hbm = refs[:groups], refs[groups:2 * groups]
    state_hbm, density_hbm, energy_ref = refs[2 * groups:2 * groups + 3]
    table_ref, start_ref, res_ref, deep_ref, state_ref, density_ref, spread, sems = refs[2 * groups + 3:]
    live = live_ref[0, 0]
    tables = [
        pltpu.make_async_copy(all_hbm, table_ref.at[pl.ds(0, sectors)], sems.at[0, 0]),
        pltpu.make_async_copy(own_hbm.at[pl.ds(0, 8)], table_ref.at[pl.ds(sectors, 8)], sems.at[1, 0]),
    ]
    coming = [pltpu.make_async_copy(start_hbm, start_ref, sems.at[2, 0])]
    for group in range(groups):
        rows = pl.ds(group * GROUPED, GROUPED)
        coming.append(pltpu.make_async_copy(res_hbm[group], res_ref.at[rows], sems.at[0, 1 + group]))
        coming.append(pltpu.make_async_copy(deep_hbm[group], deep_ref.at[rows], sems.at[1, 1 + group]))
    for copy in tables + coming:
        copy.start()
    for copy in tables:
        copy.wait()
    table = table_ref[...]
    shape = (sectors + 8, BLK)
    row = lax.broadcasted_iota(jnp.int32, shape, 0)
    lane = lax.broadcasted_iota(jnp.int32, shape, 1)
    counted = jnp.logical_and(row < sectors, lane < STRIDE)

    def pick(quantity):
        return table if quantity == 0 else pltpu.roll(table, BLK - quantity * STRIDE, 1)

    def region_sum(x):
        return total(jnp.where(counted, x, 0.0))

    norm, shift, res_norm, back, diag, deep_norm, on_f, on_r, on_d = [pick(k) for k in range(9)]
    grams = (norm, res_norm, deep_norm)
    zero = jnp.zeros(shape, jnp.float32)

    def inner(x, y):
        made = x[0] * y[0] * grams[0]
        for k in (1, 2):
            made = made + x[k] * y[k] * grams[k]
        if len(y) > 3:
            made = made + y[3] * (x[0] * on_f + x[1] * on_r + x[2] * on_d)
        return region_sum(made)

    inverse = lax.rsqrt(region_sum(norm) + EPS)
    current = (zero + inverse, zero, zero)
    applied = (inverse * shift, zero + inverse, zero)
    for iteration in range(DAV):
        quotient = inner(current, applied)
        residual = tuple(x - quotient * y for x, y in zip(applied, current))
        resid_sq = inner(residual, residual)
        factor = lax.rsqrt(resid_sq + EPS)
        search = tuple(factor * x for x in residual)
        image = (search[0] * shift + search[1] * back, search[0] + search[1] * diag, search[1])
        if iteration == 1:
            image = image + (search[2],)
        curvature = inner(search, image)
        opposite = -2.0 * resid_sq * factor
        adjacent = curvature - quotient
        largest = jnp.maximum(jnp.abs(opposite), jnp.abs(adjacent))
        flat = largest == 0.0
        largest = jnp.where(flat, 1.0, largest)
        opposite = opposite / largest
        adjacent = jnp.where(flat, 1.0, adjacent / largest)
        length = jnp.sqrt(opposite * opposite + adjacent * adjacent)
        double_cos = jnp.abs(adjacent) / length
        double_sin = jnp.abs(opposite) / length
        large = jnp.sqrt(0.5 + 0.5 * double_cos)
        small = double_sin / (2.0 * large)
        ahead = adjacent >= 0.0
        cos_part = jnp.where(ahead, large, small)
        sin_part = -jnp.where(ahead, small, large)
        current = tuple(cos_part * x + sin_part * y for x, y in zip(current, search))
        turned = tuple(cos_part * x + sin_part * y for x, y in zip(applied, image))
        applied = turned + tuple(sin_part * y for y in image[3:])
    energy_ref[...] = jnp.broadcast_to(inner(current, applied), energy_ref.shape)
    mine = [scale * x[sectors:sectors + 1, :] for x in current]
    for copy in coming:
        copy.wait()
    going = []
    for slot in range(slots):
        on_first, on_res, on_deep = [x[:, slot:slot + 1] for x in mine]
        state = on_first * start_ref[slot].astype(jnp.float32)
        state = state + on_res * res_ref[slot] + on_deep * deep_ref[slot]
        state = jnp.where(slot < live, state, 0.0).astype(jnp.bfloat16)
        state_ref[slot] = state
        spread[slot] = state.astype(jnp.float32)
        going.append(pltpu.make_async_copy(state_ref.at[slot], state_hbm.at[slot], sems.at[3, slot]))
        going[-1].start()
    for slot in range(slots):
        wide = jnp.concatenate(
            [spread[slot, pl.ds(s, BLK, stride=PHYS), :] for s in range(PHYS)], axis=1
        ).astype(jnp.bfloat16)
        product = lax.dot_general(
            wide, wide, (((1,), (1,)), ((), ())), preferred_element_type=jnp.float32
        )
        density_ref[slot] = product * (1.0 / ROWS)
        going.append(pltpu.make_async_copy(density_ref.at[slot], density_hbm.at[slot], sems.at[4, slot]))
        going[-1].start()
    for copy in going:
        copy.wait()


def from_behind(shard, axis, by):
    length = lax.axis_size(axis)
    return lax.ppermute(shard, axis, [(i, i + by) for i in range(length - by)])


def entering(decay, terms, axis):
    slots = decay.shape[0]
    own = jnp.concatenate([decay, terms], axis=0)
    other = lax.ppermute(own, axis, [(i, i ^ 1) for i in range(lax.axis_size(axis))])
    second = lax.axis_index(axis) % 2 == 1
    early, late = jnp.where(second, other, own), jnp.where(second, own, other)
    pair = jnp.concatenate(
        [early[:slots] * late[:slots], late[:slots] * early[slots:] + late[slots:]], axis=0
    )
    total = jnp.zeros_like(terms)
    for by in (6, 4, 2):
        earlier = from_behind(pair, axis, by)
        total = earlier[:slots] * total + earlier[slots:]
    return jnp.where(second, early[:slots] * total + early[slots:], total)


SMEM = pl.BlockSpec(memory_space=pltpu.SMEM)
VMEM = pl.BlockSpec(memory_space=pltpu.VMEM)
HBM = pl.BlockSpec(memory_space=pl.ANY)


def krylov_call(base, copies, live_count, region, before, offsets, operator, start, own, left, right, lanes):
    vectors = jax.ShapeDtypeStruct((GROUPED, ROWS, BLK), jnp.float32)
    head = base == 0
    kernel = functools.partial(krylov_kernel, base)
    operands = [live_count, region, offsets, start, own, left, right, lanes]
    operands += list(operator) if head else [operator, before]
    shapes = [jax.ShapeDtypeStruct((copies, BLK), jnp.float32), vectors, vectors]
    shapes += [jax.ShapeDtypeStruct((256, 256), jnp.bfloat16)] if head else []
    small = [pltpu.VMEM(x.shape, x.dtype) for x in (operator if head else [before])]
    return pl.pallas_call(
        kernel,
        in_specs=[SMEM, SMEM] + [HBM] * (len(operands) - 2),
        out_specs=[VMEM] + [HBM] * (len(shapes) - 1),
        out_shape=shapes,
        scratch_shapes=[
            pltpu.VMEM((GROUPED, ROWS, BLK), jnp.bfloat16),
            pltpu.VMEM((GROUPED, CHAN, BLK, BLK), jnp.bfloat16),
            pltpu.VMEM((GROUPED, CHAN, BLK, BLK), jnp.bfloat16),
            pltpu.VMEM((4 * BLK, 4 * BLK), jnp.bfloat16),
            pltpu.VMEM((GROUPED, ROWS, BLK), jnp.float32),
            pltpu.VMEM((GROUPED, ROWS, BLK), jnp.float32),
            pltpu.VMEM((GROUPED, BLK, CHAN * BLK), jnp.bfloat16),
            pltpu.VMEM((GROUPED, 16, 256, 256), jnp.bfloat16),
            pltpu.VMEM((GROUPED, CHAN * BLK, ROWS), jnp.bfloat16),
            pltpu.VMEM((GROUPED, ROWS, BLK), jnp.float32),
            pltpu.VMEM((GROUPED, ROWS, BLK), jnp.float32),
            pltpu.VMEM(offsets.shape, jnp.float32),
            pltpu.VMEM((256, 256), jnp.bfloat16),
            pltpu.SemaphoreType.DMA((12 + GROUPED,)),
        ] + small,
        compiler_params=pltpu.CompilerParams(vmem_limit_bytes=VMEM_LIMIT),
        cost_estimate=pl.CostEstimate(flops=10**10, bytes_accessed=1 << 22, transcendentals=0),
        name="krylov",
    )(*operands)


def rotate_call(sectors, live_count, every, sums, start, res, deep):
    slots = start.shape[0]
    return pl.pallas_call(
        functools.partial(rotate_kernel, math.sqrt(slots * sectors * ROWS * BLK), slots, sectors),
        in_specs=[SMEM] + [HBM] * (3 + 2 * (slots // GROUPED)),
        out_specs=[HBM, HBM, VMEM],
        out_shape=[
            jax.ShapeDtypeStruct((slots, ROWS, BLK), jnp.bfloat16),
            jax.ShapeDtypeStruct((slots, BLK, BLK), jnp.float32),
            jax.ShapeDtypeStruct((1, 1), jnp.float32),
        ],
        scratch_shapes=[
            pltpu.VMEM((sectors + 8, BLK), jnp.float32),
            pltpu.VMEM((slots, ROWS, BLK), jnp.bfloat16),
            pltpu.VMEM((slots, ROWS, BLK), jnp.float32),
            pltpu.VMEM((slots, ROWS, BLK), jnp.float32),
            pltpu.VMEM((slots, ROWS, BLK), jnp.bfloat16),
            pltpu.VMEM((slots, BLK, BLK), jnp.float32),
            pltpu.VMEM((slots, ROWS, BLK), jnp.float32),
            pltpu.SemaphoreType.DMA((5, slots)),
        ],
        compiler_params=pltpu.CompilerParams(vmem_limit_bytes=VMEM_LIMIT),
        name="rotate",
    )(live_count, every, sums, start, *res, *deep)


def body(start_state, left_env, right_env, mpo_tensor, decay, energy_terms, live_count):
    slots = start_state.shape[1]
    sectors = lax.axis_size("sector")
    start = start_state.reshape(slots, ROWS, BLK)
    arrived = [from_behind(left_env[0, at:at + GROUPED], "region", 1) for at in range(0, slots, GROUPED)]
    offsets = entering(decay[0], energy_terms[0], "region")
    region = lax.axis_index("region").reshape(1).astype(jnp.int32)
    mpo = mpo_tensor.reshape(CHAN * PHYS, PHYS * CHAN)
    lanes, rows, cols, same = constants()
    sums = None
    operator = (mpo, rows, cols, same)
    res, deep = [], []
    for base in range(0, slots, GROUPED):
        copies = sectors if base + GROUPED == slots else 1
        sums, res_one, deep_one, *made = krylov_call(
            base, copies, live_count, region, sums, offsets, operator,
            start, left_env[0], arrived[base // GROUPED], right_env[0], lanes,
        )
        operator = made[0] if made else operator
        res.append(res_one)
        deep.append(deep_one)
    every = lax.all_to_all(sums.reshape(sectors, 1, BLK), "sector", 0, 0).reshape(sectors, BLK)
    state, density, energy = rotate_call(sectors, live_count, every, sums, start, res, deep)
    return (state.reshape(start_state.shape), density[None], energy.reshape(1))


def solution(mesh):
    in_specs = (
        P("region", "sector", None, None, None),
        P("region", "sector", None, None, None),
        P("region", "sector", None, None, None),
        P(),
        P("region", "sector", None),
        P("region", "sector", None),
        P("region", "sector"),
    )
    out_specs = (
        P("region", "sector", None, None, None),
        P("region", "sector", None, None),
        P("region"),
    )
    return jax.shard_map(body, mesh=mesh, in_specs=in_specs, out_specs=out_specs, check_vma=False)
```
